32 devices in a mesh: groups: 2 (over y), dp: 4 (over z), expert: 2 (over x), tensor: 2 (over core).
Axes of the slice: x: 2, y: 2, z: 4, core: 2. Of those that a mesh axis runs over, the one named last changes fastest.
Arguments:
- tokens: bfloat16 [512, 3072], P(('groups', 'expert'), ('tensor', 'dp')), parts along dimension 0, may hold values from -6 to 6
- cotangent: bfloat16 [512, 3072], P(('groups', 'expert'), ('tensor', 'dp')), parts along dimension 0, may hold values from -6 to 6
- expert_ids: int32 [512, 2], P(('groups', 'expert')), parts along dimension 0, may hold values from 0 to 3, all different within a row; in each aligned block of 128 rows (0 to 127, 128 to 255, ...) at most 80 rows name the same one
- gate_values: bfloat16 [512, 2], P(('groups', 'expert')), parts along dimension 0, may hold values from 0.19921875 to 1
- gate_weight: bfloat16 [3072, 32768], P('tensor', ('expert', 'dp')), may hold values from -0.109375 to 0.109375
- up_weight: bfloat16 [3072, 32768], P('tensor', ('expert', 'dp')), may hold values from -0.109375 to 0.109375
- down_weight: bfloat16 [3072, 32768], P('tensor', ('expert', 'dp')), may hold values from -0.109375 to 0.109375
Outputs:
- token_grad: bfloat16 [512, 3072], P(('groups', 'expert'), ('tensor', 'dp')), parts along dimension 0
- gate_grad: bfloat16 [6144, 32768], P(('groups', 'tensor'), ('expert', 'dp')), parts along dimension 0
- up_grad: bfloat16 [6144, 32768], P(('groups', 'tensor'), ('expert', 'dp')), parts along dimension 0
- down_grad: bfloat16 [6144, 32768], P(('groups', 'tensor'), ('expert', 'dp')), parts along dimension 0
The draws below stay inside these ranges and needn't reach their ends.
There are 2 independent parts, one for each index of `groups`. The reference program is written for one: setup_inputs(seed, part) draws one part's arguments, and reference() takes and returns one part's arrays. A program takes and returns all parts, laid end to end along the dimension named above; an argument that names none is the same for every part. Nothing has to cross between parts.
Inputs may be any that keep to these rules, and one draw needn't show every extreme that they name: `expert_ids`: each token names two different experts. Within each block of 128 rows (the rows of one index of expert) no expert is named more than 80 times, a bound that some block reaches.
All inputs are finite; a program needn't handle non-finite values.
Results may differ from the reference program's by a relative error of at most 0.019.
Values may be sent and summed in bfloat16 or wider, within the bound.
No kernel may reach another device: no remote copies, remote signals or barrier semaphores. Data moves between devices by JAX's collectives and lax.ppermute only.
A program may use at most 192 MiB of HBM per device.

```python
import math
import jax
import jax.numpy as jnp
import numpy as np
from jax import lax

D = 3072
FF = 8192
EXPERTS = 4
TOK_DEV = 128
CAP = 80
TOKENS = 256
HB = 4096
N_EXPERT = 2


def level_of(key, dims, cuts, low, top_value):
    def one(dim, shards_of):
        draws = jax.random.uniform(jax.random.fold_in(jax.random.fold_in(key, 6), dim), (shards_of,), jnp.float32, low / len(cuts), top_value / len(cuts))
        return jnp.repeat(jnp.exp(draws), dims[dim] // shards_of).reshape((-1,) + (1,) * (len(dims) - dim - 1))

    factor_of = one(*cuts[0])
    for cut in cuts[1:]:
        factor_of = factor_of * one(*cut)
    return factor_of


def routed_block(stream_key, own, number, rows, count, top, limit, slope):
    order = jax.random.permutation(stream_key, count)
    packed, usual = load_shares(count, rows * top, limit, slope, True), load_shares(count, rows * top, limit, slope, False)
    places = jnp.arange(count)

    def named(sizes, offset_by):
        used = int((sizes > 0).sum())
        fixed = max(1, used // 4)
        shifted = fixed + (places - fixed + offset_by * (used - fixed)) % max(1, count - fixed)
        return jnp.zeros((count,), jnp.int32).at[order[jnp.where(places < fixed, places, shifted)]].set(jnp.asarray(sizes, jnp.int32))

    sizes = jnp.where(number % 4 == 0, named(packed, number // 4), named(usual, number - number // 4 - 1))
    mixed = jax.random.permutation(jax.random.fold_in(own, 3), count)
    donor, sink = mixed[0:count // 2 * 2:2], mixed[1:count // 2 * 2:2]
    margin = jnp.minimum(sizes[donor] - 1, limit - sizes[sink]) // 2
    margin = jnp.where((donor == order[0]) | (sink == order[0]) | (sizes[sink] == 0), 0, jnp.maximum(margin, 0))
    shifted = jax.random.randint(jax.random.fold_in(own, 4), (count // 2,), 0, 1 << 20) % (margin + 1)
    sizes = sizes.at[donor].add(-shifted).at[sink].add(shifted)
    members = jnp.searchsorted(jnp.cumsum(sizes), jnp.arange(rows * top), side="right").astype(jnp.int32)
    listing = members.reshape(top, rows).T
    listing = listing[jax.random.permutation(jax.random.fold_in(own, 1), rows)]
    offset_by = jax.random.randint(jax.random.fold_in(own, 2), (rows, 1), 0, top)
    return jnp.take_along_axis(listing, (jnp.arange(top)[None, :] + offset_by) % top, axis=1)


def load_shares(number_of, total, bound, slope, full):
    portions = [(1 << 20) // math.isqrt(rank ** slope) + 1 for rank in range(1, number_of + 1)]
    largest = bound if full else min(bound, max(-(-total // number_of), total * portions[0] // sum(portions)))
    least = 1 if total - largest >= number_of - 1 else 0
    holding, rest = [largest] + [least] * (number_of - 1), total - largest - least * (number_of - 1)
    while rest > 0:
        free = [i for i in range(1, number_of) if holding[i] < largest] or [i for i in range(1, number_of) if holding[i] < bound]
        pool, left = sum([portions[i] for i in free]), rest
        for i in free:
            addition = min(bound - holding[i], max(1, left * portions[i] // pool), rest)
            holding[i] = holding[i] + addition
            rest = rest - addition
    return np.array(holding)


def centred(rng, extent, deviation, limit, cuts=(), kind=jnp.bfloat16):
    level = level_of(rng, extent, cuts, -0.22, 0.18) if cuts else 1.0
    entries = jax.random.normal(rng, extent, jnp.float32) * deviation * level
    return jnp.minimum(jnp.maximum(entries, -limit), limit).astype(kind)


def setup_inputs(seed: int = 0, part: int = 0) -> dict:
    streams_of = jax.random.split(jax.random.key(seed), 8)
    part_splits = jax.random.split(jax.random.fold_in(streams_of[7], part), 8)
    tokens = centred(part_splits[0], (TOKENS, D), 1.0, 6.0, ((0, 2), (1, 8)))
    cotangent = centred(part_splits[1], (TOKENS, D), 1.0, 6.0, ((0, 2), (1, 8)))
    expert_ids_keys = jax.random.split(jax.random.fold_in(part_splits[2], 1), TOKENS // TOK_DEV)
    expert_ids_turns = jax.random.permutation(jax.random.fold_in(part_splits[2], 3), TOKENS // TOK_DEV)
    expert_ids = jax.vmap(lambda own, number: routed_block(jax.random.fold_in(part_splits[2], 2), own, number, TOK_DEV, EXPERTS, 2, CAP, 2))(expert_ids_keys, expert_ids_turns).reshape((TOKENS, 2))
    gate_values = jnp.clip(0.19921875 + 0.80078125 * jax.random.uniform(part_splits[3], (TOKENS, 2), jnp.float32) ** level_of(part_splits[3], (TOKENS, 2), ((0, 2),), -0.2, 0.2), 0.19921875, 1.0).astype(jnp.bfloat16)
    gate_weight = centred(streams_of[4], (D, EXPERTS * FF), D ** -0.5, 0.109375, ((0, 2), (1, 8)))
    up_weight = centred(streams_of[5], (D, EXPERTS * FF), D ** -0.5, 0.109375, ((0, 2), (1, 8)))
    down_weight = centred(streams_of[6], (D, EXPERTS * FF), D ** -0.5, 0.109375, ((0, 2), (1, 8)))
    return {"tokens": tokens, "cotangent": cotangent, "expert_ids": expert_ids, "gate_values": gate_values, "gate_weight": gate_weight, "up_weight": up_weight, "down_weight": down_weight}


def slots(ids):
    flat = ids.reshape(-1)
    onehot = (flat[:, None] == jnp.arange(EXPERTS, dtype=jnp.int32)[None, :]).astype(jnp.int32)
    before = jnp.cumsum(onehot, axis=0) - onehot
    return (flat * CAP + lax.optimization_barrier(jnp.sum(before * onehot, axis=1))).astype(jnp.int32)

def place(values, dest):
    return jnp.zeros((EXPERTS * CAP, D), jnp.bfloat16).at[dest].set(values)

def block_sum(d_gate, d_up, w_gate, w_up):

    def add_block(index, total):
        start = (index * HB).astype(jnp.int32)
        gate_cols = lax.dynamic_slice_in_dim(d_gate, start, HB, 1)
        up_cols = lax.dynamic_slice_in_dim(d_up, start, HB, 1)
        gate_rows = lax.dynamic_slice_in_dim(w_gate, start, HB, 1)
        up_rows = lax.dynamic_slice_in_dim(w_up, start, HB, 1)
        term = jnp.dot(gate_cols, gate_rows.T, preferred_element_type=jnp.float32)
        term = term + jnp.dot(up_cols, up_rows.T, preferred_element_type=jnp.float32)
        rounded = lax.optimization_barrier(term.astype(jnp.bfloat16))
        return total + rounded.astype(jnp.float32)
    return lax.fori_loop(0, FF // HB, add_block, jnp.zeros((d_gate.shape[0], D), jnp.float32))

def reference(tokens, cotangent, expert_ids, gate_values, gate_weight, up_weight, down_weight):
    x_all = tokens.reshape(N_EXPERT, TOK_DEV, D)
    dy_all = cotangent.reshape(N_EXPERT, TOK_DEV, D)
    ids_all = expert_ids.reshape(N_EXPERT, TOK_DEV, 2)
    gates_all = gate_values.reshape(N_EXPERT, TOK_DEV * 2)
    dest = jax.vmap(slots)(ids_all)
    scaled = (gates_all.astype(jnp.float32)[..., None] * jnp.repeat(dy_all, 2, axis=1).astype(jnp.float32)).astype(jnp.bfloat16)
    x_buf = jax.vmap(place)(jnp.repeat(x_all, 2, axis=1), dest).reshape(N_EXPERT, EXPERTS, CAP, D)
    q_buf = jax.vmap(place)(scaled, dest).reshape(N_EXPERT, EXPERTS, CAP, D)
    factor = 1.0 / math.sqrt(TOKENS)
    pieces = []
    gate_grads = []
    up_grads = []
    down_grads = []
    for expert in range(EXPERTS):
        w_gate = gate_weight[:, expert * FF:(expert + 1) * FF]
        w_up = up_weight[:, expert * FF:(expert + 1) * FF]
        w_down = down_weight[:, expert * FF:(expert + 1) * FF]
        rows_x = x_buf[:, expert].reshape(N_EXPERT * CAP, D)
        rows_q = q_buf[:, expert].reshape(N_EXPERT * CAP, D)
        pre_gate = jnp.dot(rows_x, w_gate, preferred_element_type=jnp.float32)
        pre_up = jnp.dot(rows_x, w_up, preferred_element_type=jnp.float32)
        d_hidden = jnp.dot(rows_q, w_down, preferred_element_type=jnp.float32)
        sigma = jax.nn.sigmoid(pre_gate)
        act = sigma * pre_gate
        hidden = (act * pre_up).astype(jnp.bfloat16)
        d_gate = (d_hidden * pre_up * sigma * (1.0 + pre_gate * (1.0 - sigma))).astype(jnp.bfloat16)
        d_up = (d_hidden * act).astype(jnp.bfloat16)
        pieces.append(block_sum(d_gate, d_up, w_gate, w_up).reshape(N_EXPERT, CAP, D))
        gate_grads.append((jnp.dot(rows_x.T, d_gate, preferred_element_type=jnp.float32) * factor).astype(jnp.bfloat16))
        up_grads.append((jnp.dot(rows_x.T, d_up, preferred_element_type=jnp.float32) * factor).astype(jnp.bfloat16))
        down_grads.append((jnp.dot(rows_q.T, hidden, preferred_element_type=jnp.float32) * factor).astype(jnp.bfloat16))
    back_buf = jnp.stack(pieces, axis=1).reshape(N_EXPERT, EXPERTS * CAP, D)
    back = jax.vmap(lambda buf, where: buf[where])(back_buf, dest)
    token_grad = back.reshape(N_EXPERT, TOK_DEV, 2, D).sum(axis=2).astype(jnp.bfloat16).reshape(TOKENS, D)
    return (token_grad, jnp.concatenate(gate_grads, axis=1), jnp.concatenate(up_grads, axis=1), jnp.concatenate(down_grads, axis=1))
```

```python
import functools
import math

import jax
import jax.numpy as jnp
from jax import lax
from jax.experimental import pallas as pl
from jax.experimental.pallas import tpu as pltpu
from jax.sharding import PartitionSpec as P

FF = 8192
EXPERTS = 4
CAP = 80
F32 = jnp.float32
BF16 = jnp.bfloat16
VMEM_LIMIT = 48 * 1024 * 1024


def params():
    return pltpu.CompilerParams(vmem_limit_bytes=VMEM_LIMIT)


def cost(flops, moved):
    return pl.CostEstimate(flops=flops, bytes_accessed=moved, transcendentals=0)


def is_pow2(value):
    return value & (value - 1) == 0


def block_of(size, wanted):
    while size % wanted:
        wanted //= 2
    return wanted


class Plan:
    def __init__(self, mesh, columns):
        self.owners = mesh.shape["expert"]
        self.replicas = mesh.shape["dp"]
        self.partners = self.owners * self.replicas
        self.direct = self.partners <= 8 and is_pow2(self.owners) and is_pow2(self.replicas)
        self.columns = columns
        self.refs, self.each = (self.partners, 1) if self.direct else (1, self.partners)

    def width_index(self, j, z):
        dz = j % self.replicas
        return jnp.bitwise_xor(z, dz) if self.direct else dz

    def expert_of(self, j, x, z):
        if self.direct:
            device = jnp.bitwise_xor(x, j // self.replicas) * self.replicas + jnp.bitwise_xor(z, j % self.replicas)
        else:
            device = j
        return device * self.columns // FF

    def exchange(self, sends):
        if not self.direct:
            return [lax.all_to_all(sends[0], ("expert", "dp"), 0, 0, tiled=True)]
        out = [sends[0]]
        for j in range(1, self.partners):
            dx, dz = j // self.replicas, j % self.replicas
            pairs = []
            for x in range(self.owners):
                for z in range(self.replicas):
                    pairs.append((z * self.owners + x, (z ^ dz) * self.owners + (x ^ dx)))
            out.append(lax.ppermute(sends[j], ("dp", "expert"), pairs))
        return out


def dispatch_kernel(plan, where_ref, ids_ref, gates_ref, tok_ref, cot_ref, *outs):
    n = plan.refs
    x_refs, q_refs, sel_ref = outs[:n], outs[n:2 * n], outs[2 * n]
    x_at, z_at = where_ref[0], where_ref[1]
    count = tok_ref.shape[0]
    first, second = ids_ref[0:1, :], ids_ref[1:2, :]
    gate_first, gate_second = gates_ref[0:1, :].astype(F32), gates_ref[1:2, :].astype(F32)
    row = lax.broadcasted_iota(jnp.int32, (16, count), 0)
    named = ((row == first) | (row == second)).astype(F32)
    earlier = lax.broadcasted_iota(jnp.int32, (count, count), 0) < lax.broadcasted_iota(jnp.int32, (count, count), 1)
    before = jnp.dot(named.astype(BF16), earlier.astype(F32).astype(BF16), preferred_element_type=F32)
    slot = lax.broadcasted_iota(jnp.int32, (CAP, count), 0).astype(F32)
    tok, cot = tok_ref[...], cot_ref[...]

    def one(ref_index, inner, j):
        expert = plan.expert_of(j, x_at, z_at)
        mine = (row == expert).astype(F32)
        position = jnp.sum(mine * before, axis=0, keepdims=True)
        here = jnp.sum(mine * named, axis=0, keepdims=True)
        chosen = jnp.where((position == slot) & (here > 0.5), 1.0, 0.0)
        gate = jnp.where(first == expert, gate_first, gate_second)
        weight = jnp.sum(chosen * gate, axis=1, keepdims=True)
        chosen = chosen.astype(BF16)
        x_refs[ref_index][inner] = jnp.dot(chosen, tok, preferred_element_type=F32).astype(BF16)
        q_refs[ref_index][inner] = (weight * jnp.dot(chosen, cot, preferred_element_type=F32)).astype(BF16)
        sel_ref[j] = chosen

    if plan.direct:
        for j in range(n):
            one(j, 0, j)
    else:
        lax.fori_loop(0, plan.each, lambda j, c: (one(0, j, j), c)[1], 0)


def dispatch(plan, where, ids, gates, tokens, cotangent):
    count, narrow = tokens.shape
    piece = jax.ShapeDtypeStruct((plan.each, CAP, narrow), BF16)
    vmem = pl.BlockSpec(memory_space=pltpu.VMEM)
    outs = pl.pallas_call(
        functools.partial(dispatch_kernel, plan),
        out_shape=[piece] * (2 * plan.refs) + [jax.ShapeDtypeStruct((plan.partners, CAP, count), BF16)],
        in_specs=[pl.BlockSpec(memory_space=pltpu.SMEM)] + [vmem] * 4,
        out_specs=[vmem] * (2 * plan.refs + 1),
        compiler_params=params(),
        name="dispatch",
    )(where, ids.T, gates.T, tokens, cotangent)
    return outs[: plan.refs], outs[plan.refs : 2 * plan.refs], outs[-1]


def lanes(plan, j, z, narrow):
    start = plan.width_index(j, z) * narrow
    if plan.direct:
        start = pl.multiple_of(start, 128)
    return pl.ds(start, narrow)


def forward_kernel(plan, weights, where_ref, *refs):
    pieces, w_refs = refs[: plan.refs], refs[plan.refs : plan.refs + weights]
    full_ref, part_refs = refs[plan.refs + weights], refs[plan.refs + weights + 1 :]
    narrow = pieces[0].shape[2]

    @pl.when(pl.program_id(0) == 0)
    def _():
        for j in range(plan.partners):
            rows = pl.ds(j // plan.replicas * CAP, CAP)
            full_ref[rows, lanes(plan, j, where_ref[1], narrow)] = pieces[j // plan.each][j % plan.each]

    for w_ref, part_ref in zip(w_refs, part_refs):
        part_ref[...] = jnp.dot(full_ref[...], w_ref[...], preferred_element_type=F32).astype(BF16)


def forward(plan, where, pieces, weights, name, wanted=512):
    width, columns = weights[0].shape
    rows, block = plan.owners * CAP, block_of(columns, wanted)
    part = jax.ShapeDtypeStruct((rows, columns), BF16)
    whole = pl.BlockSpec(memory_space=pltpu.VMEM)
    resident = pl.BlockSpec((rows, width), lambda i: (0, 0))
    strip = pl.BlockSpec((width, block), lambda i: (0, i))
    part_spec = pl.BlockSpec((rows, block), lambda i: (0, i))
    k = len(weights)
    return pl.pallas_call(
        functools.partial(forward_kernel, plan, k),
        grid=(columns // block,),
        out_shape=[jax.ShapeDtypeStruct((rows, width), BF16)] + [part] * k,
        in_specs=[pl.BlockSpec(memory_space=pltpu.SMEM)] + [whole] * plan.refs + [strip] * k,
        out_specs=[resident] + [part_spec] * k,
        compiler_params=params(),
        cost_estimate=cost(2 * k * rows * width * columns, 2 * k * width * columns),
        name=name,
    )(where, *pieces, *weights)


def rows_kernel(plan, where_ref, g0, g1, u0, u1, d0, d1, wg_ref, wu_ref, h_ref, dg_ref, du_ref, *rest):
    outs, total = rest[: plan.refs], rest[plan.refs]
    gate = g0[...].astype(F32) + g1[...].astype(F32)
    up = u0[...].astype(F32) + u1[...].astype(F32)
    hidden = d0[...].astype(F32) + d1[...].astype(F32)
    sigma = jax.nn.sigmoid(gate)
    act = sigma * gate
    h_ref[...] = (act * up).astype(BF16)
    d_gate = (hidden * up * sigma * (1.0 + gate * (1.0 - sigma))).astype(BF16)
    d_up = (hidden * act).astype(BF16)
    dg_ref[...] = d_gate
    du_ref[...] = d_up
    turned = (((1,), (1,)), ((), ()))
    term = lax.dot_general(d_gate, wg_ref[...], turned, preferred_element_type=F32)
    term = term + lax.dot_general(d_up, wu_ref[...], turned, preferred_element_type=F32)
    step = pl.program_id(0)

    @pl.when(step == 0)
    def _():
        total[...] = term

    @pl.when(step > 0)
    def _():
        total[...] += term

    @pl.when(step == pl.num_programs(0) - 1)
    def _():
        narrow = outs[0].shape[2]
        for j in range(plan.partners):
            rows = pl.ds(j // plan.replicas * CAP, CAP)
            outs[j // plan.each][j % plan.each] = total[rows, lanes(plan, j, where_ref[1], narrow)].astype(BF16)


def row_grads(plan, where, parts, wg, wu, wanted=512):
    width, columns = wg.shape
    narrow = width // plan.replicas
    rows, block = plan.owners * CAP, block_of(columns, wanted)
    strip = pl.BlockSpec((width, block), lambda i: (0, i))
    part_spec = pl.BlockSpec((rows, block), lambda i: (0, i))
    piece = jax.ShapeDtypeStruct((plan.each, CAP, narrow), BF16)
    hidden = jax.ShapeDtypeStruct((rows, columns), BF16)
    outs = pl.pallas_call(
        functools.partial(rows_kernel, plan),
        grid=(columns // block,),
        out_shape=[hidden] * 3 + [piece] * plan.refs,
        in_specs=[pl.BlockSpec(memory_space=pltpu.SMEM)] + [part_spec] * 6 + [strip] * 2,
        out_specs=[part_spec] * 3 + [pl.BlockSpec((plan.each, CAP, narrow), lambda i: (0, 0, 0))] * plan.refs,
        scratch_shapes=[pltpu.VMEM((rows, width), F32)],
        compiler_params=params(),
        cost_estimate=cost(4 * rows * width * columns, 4 * width * columns),
        name="row_grads",
    )(where, *parts, wg, wu)
    return outs[:3], outs[3:]


def weights_kernel(factor, x_ref, q_ref, dg_ref, du_ref, h_ref, gg_ref, gu_ref, gd_ref):
    turned = (((0,), (0,)), ((), ()))
    for rows_ref, d_ref, out_ref in ((x_ref, dg_ref, gg_ref), (x_ref, du_ref, gu_ref), (q_ref, h_ref, gd_ref)):
        grad = lax.dot_general(rows_ref[...], d_ref[...], turned, preferred_element_type=F32)
        out_ref[...] = (grad * factor).astype(BF16)


def weight_grads(factor, x_full, q_full, hidden, wanted=512):
    rows, width = x_full.shape
    columns = hidden[0].shape[1]
    block = block_of(columns, wanted)
    resident = pl.BlockSpec((rows, width), lambda i: (0, 0))
    part_spec = pl.BlockSpec((rows, block), lambda i: (0, i))
    out_spec = pl.BlockSpec((width, block), lambda i: (0, i))
    return pl.pallas_call(
        functools.partial(weights_kernel, factor),
        grid=(columns // block,),
        out_shape=[jax.ShapeDtypeStruct((width, columns), BF16)] * 3,
        in_specs=[resident] * 2 + [part_spec] * 3,
        out_specs=[out_spec] * 3,
        compiler_params=params(),
        cost_estimate=cost(6 * rows * width * columns, 6 * width * columns),
        name="weight_grads",
    )(x_full, q_full, *hidden)


def combine_kernel(plan, sel_ref, *rest):
    backs, out_ref = rest[: plan.refs], rest[plan.refs]
    turned = (((0,), (0,)), ((), ()))

    def term(ref, inner, j):
        return lax.dot_general(sel_ref[j], ref[inner], turned, preferred_element_type=F32)

    if plan.direct:
        total = term(backs[0], 0, 0)
        for j in range(1, plan.refs):
            total = total + term(backs[j], 0, j)
    else:
        total = lax.fori_loop(0, plan.each, lambda j, t: t + term(backs[0], j, j), jnp.zeros(out_ref.shape, F32))
    out_ref[...] = total.astype(BF16)


def combine(plan, sel, backs):
    count, narrow = sel.shape[2], backs[0].shape[2]
    vmem = pl.BlockSpec(memory_space=pltpu.VMEM)
    return pl.pallas_call(
        functools.partial(combine_kernel, plan),
        out_shape=jax.ShapeDtypeStruct((count, narrow), BF16),
        in_specs=[vmem] * (1 + plan.refs),
        out_specs=vmem,
        compiler_params=params(),
        name="combine",
    )(sel, *backs)


def body(mesh, tokens, cotangent, expert_ids, gate_values, gate_weight, up_weight, down_weight):
    plan = Plan(mesh, gate_weight.shape[1])
    where = jnp.stack((lax.axis_index("expert"), lax.axis_index("dp"))).astype(jnp.int32)
    x_send, q_send, sel = dispatch(plan, where, expert_ids, gate_values, tokens, cotangent)
    x_pieces = plan.exchange(x_send)
    q_pieces = plan.exchange(q_send)

    def swap(part):
        size = mesh.shape["tensor"]
        return lax.ppermute(part, "tensor", [(i, i ^ 1) for i in range(size)])

    x_full, part_g, part_u = forward(plan, where, x_pieces, [gate_weight, up_weight], "forward_gu")
    other_g, other_u = swap(part_g), swap(part_u)
    q_full, part_h = forward(plan, where, q_pieces, [down_weight], "forward_h")
    other_h = swap(part_h)
    hidden, pieces = row_grads(plan, where, (part_g, other_g, part_u, other_u, part_h, other_h), gate_weight, up_weight)
    (h, d_gate, d_up) = hidden
    backs = plan.exchange(pieces)
    factor = 1.0 / math.sqrt(tokens.shape[0] * plan.owners)
    grads = weight_grads(factor, x_full, q_full, (d_gate, d_up, h))
    token_grad = combine(plan, sel, backs)
    return (token_grad, *grads)


def solution(mesh):
    in_specs = (
        P(("groups", "expert"), ("tensor", "dp")),
        P(("groups", "expert"), ("tensor", "dp")),
        P(("groups", "expert"), None),
        P(("groups", "expert"), None),
        P("tensor", ("expert", "dp")),
        P("tensor", ("expert", "dp")),
        P("tensor", ("expert", "dp")),
    )
    out_specs = (
        P(("groups", "expert"), ("tensor", "dp")),
        P(("groups", "tensor"), ("expert", "dp")),
        P(("groups", "tensor"), ("expert", "dp")),
        P(("groups", "tensor"), ("expert", "dp")),
    )
    return jax.shard_map(
        functools.partial(body, mesh), mesh=mesh, in_specs=in_specs, out_specs=out_specs, check_vma=False
    )
```

```python
import functools
import math

import jax
import jax.numpy as jnp
from jax import lax
from jax.experimental import pallas as pl
from jax.experimental.pallas import tpu as pltpu
from jax.sharding import PartitionSpec as P

FF = 8192
EXPERTS = 4
CAP = 80
F32 = jnp.float32
BF16 = jnp.bfloat16
PARTNERS = ((0, 0), (1, 0), (0, 2), (1, 2))
TURNED = (((1,), (1,)), ((), ()))
BOTH_FIRST = (((0,), (0,)), ((), ()))
VMEM = pl.BlockSpec(memory_space=pltpu.VMEM)
SMEM = pl.BlockSpec(memory_space=pltpu.SMEM)
ANY = pl.BlockSpec(memory_space=pl.ANY)
HBM = pl.BlockSpec(memory_space=pltpu.HBM)


def params(mebibytes):
    return pltpu.CompilerParams(vmem_limit_bytes=mebibytes * 1024 * 1024)


def cost(flops, moved):
    return pl.CostEstimate(flops=flops, bytes_accessed=moved, transcendentals=0)


def block_of(size, wanted):
    while size % wanted:
        wanted //= 2
    return wanted


class Plan:
    def __init__(self, mesh, columns):
        self.owners = mesh.shape["expert"]
        self.replicas = mesh.shape["dp"]
        self.devices = self.owners * self.replicas
        self.rows = self.owners * CAP
        self.columns = columns
        self.hops = self.owners == 2 and self.replicas == 4 and 2 * columns == FF

    def expert_of(self, x, z):
        return (x * self.replicas + z) * self.columns // FF

    def send(self, array, dx, dz):
        pairs = []
        for x in range(self.owners):
            for z in range(self.replicas):
                pairs.append((z * self.owners + x, (z ^ dz) * self.owners + (x ^ dx)))
        return lax.ppermute(array, ("dp", "expert"), pairs)

    def scatter(self, array):
        return lax.all_to_all(array, ("dp", "expert"), 0, 0, tiled=True)


def dispatch_kernel(plan, where_ref, ids_ref, gates_ref, tok_ref, cot_ref, sel_ref, *send_refs):
    count = tok_ref.shape[0]
    first, second = ids_ref[0:1, :], ids_ref[1:2, :]
    gate_first, gate_second = gates_ref[0:1, :].astype(F32), gates_ref[1:2, :].astype(F32)
    row = lax.broadcasted_iota(jnp.int32, (16, count), 0)
    named = ((row == first) | (row == second)).astype(F32)
    earlier = lax.broadcasted_iota(jnp.int32, (count, count), 0) < lax.broadcasted_iota(jnp.int32, (count, count), 1)
    before = jnp.dot(named.astype(BF16), earlier.astype(F32).astype(BF16), preferred_element_type=F32)
    slot = lax.broadcasted_iota(jnp.int32, (CAP, count), 0).astype(F32)

    def rows_for(expert):
        mine = row == expert
        position = jnp.sum(jnp.where(mine, before, 0.0), axis=0, keepdims=True)
        here = jnp.sum(jnp.where(mine, named, 0.0), axis=0, keepdims=True)
        chosen = jnp.where((position == slot) & (here > 0.5), 1.0, 0.0)
        gate = jnp.sum(chosen * jnp.where(first == expert, gate_first, gate_second), axis=1, keepdims=True)
        chosen = chosen.astype(BF16)
        x_rows = jnp.dot(chosen, tok_ref[...], preferred_element_type=F32).astype(BF16)
        q_rows = (gate * jnp.dot(chosen, cot_ref[...], preferred_element_type=F32)).astype(BF16)
        return chosen, x_rows, q_rows

    if plan.hops:
        for at, (dx, dz) in enumerate(PARTNERS):
            expert = plan.expert_of(jnp.bitwise_xor(where_ref[0], dx), jnp.bitwise_xor(where_ref[1], dz))
            sel_ref[at], send_refs[at][0, 0:CAP, :], send_refs[at][0, CAP : 2 * CAP, :] = rows_for(expert)
        return
    for expert in range(EXPERTS):
        chosen, x_rows, q_rows = rows_for(expert)
        sel_ref[expert] = chosen
        for z in range(plan.replicas):
            for x in range(plan.owners):
                if plan.expert_of(x, z) == expert:
                    send_refs[0][z * plan.owners + x, 0:CAP, :] = x_rows
                    send_refs[0][z * plan.owners + x, CAP : 2 * CAP, :] = q_rows


def dispatch(plan, where, ids, gates, tokens, cotangent, fetched):
    count, narrow = tokens.shape
    sends = [jax.ShapeDtypeStruct((1, 2 * CAP, narrow), BF16)] * len(PARTNERS)
    if not plan.hops:
        sends = [jax.ShapeDtypeStruct((plan.devices, 2 * CAP, narrow), BF16)]
    got = pl.pallas_call(
        functools.partial(dispatch_kernel, plan),
        out_shape=[jax.ShapeDtypeStruct((EXPERTS, CAP, count), BF16)] + sends,
        in_specs=[SMEM] + [VMEM] * 4,
        out_specs=[VMEM] * (1 + len(sends)),
        compiler_params=params(8),
        cost_estimate=cost(400 * fetched, fetched),
        name="dispatch",
    )(where, ids.T, gates.T, tokens, cotangent)
    return got[0], got[1:]


def forward_kernel(plan, half, block, *refs):
    part_ref = refs[-1]
    if half is None:
        rows_ref, w_ref = refs[:2]
    else:
        where_ref, pieces, w_ref, rows_ref = refs[0], refs[1:-3], refs[-3], refs[-2]
        narrow = pieces[0].shape[2]
        for z in range(plan.replicas):
            if plan.hops:
                index = jnp.bitwise_xor(where_ref[1], z)
                lanes = pl.ds(pl.multiple_of(index * narrow, 128), narrow)
            else:
                lanes = pl.ds(z * narrow, narrow)
            for x in range(plan.owners):
                at = z * plan.owners + x
                piece = pieces[at] if plan.hops else pieces[0].at[pl.ds(at, 1)]
                rows_ref[x * CAP : (x + 1) * CAP, lanes] = piece[0, half * CAP : (half + 1) * CAP, :]
    for start in range(0, w_ref.shape[1], block):
        cols = pl.ds(start, block)
        part_ref[:, cols] = jnp.dot(rows_ref[...], w_ref[:, cols], preferred_element_type=F32).astype(BF16)


def forward(plan, where, rows_in, half, w, name, wanted=512):
    width, columns = w.shape
    block = block_of(columns, wanted)
    fresh = half is not None
    outs = [jax.ShapeDtypeStruct((plan.rows, width), BF16)] * fresh
    outs.append(jax.ShapeDtypeStruct((plan.rows, columns), BF16))
    return pl.pallas_call(
        functools.partial(forward_kernel, plan, half, block),
        out_shape=outs,
        in_specs=[SMEM] * fresh + [VMEM] * (1 + len(rows_in)),
        out_specs=[VMEM] * len(outs),
        compiler_params=params(4),
        cost_estimate=cost(2 * plan.rows * width * columns, 8 * 1024 * 1024),
        name=name,
    )(*([where] * fresh), *rows_in, w)


def rows_kernel(plan, where_ref, g0, g1, u0, u1, d0, d1, wg_ref, wu_ref, h_ref, dg_ref, du_ref, *rest):
    outs, total = rest[:-1], rest[-1]
    gate = g0[...].astype(F32) + g1[...].astype(F32)
    up = u0[...].astype(F32) + u1[...].astype(F32)
    hidden = d0[...].astype(F32) + d1[...].astype(F32)
    sigma = jax.nn.sigmoid(gate)
    act = sigma * gate
    h_ref[...] = (act * up).astype(BF16)
    d_gate = (hidden * up * sigma * (1.0 + gate * (1.0 - sigma))).astype(BF16)
    d_up = (hidden * act).astype(BF16)
    dg_ref[...] = d_gate
    du_ref[...] = d_up
    term = lax.dot_general(d_gate, wg_ref[...], TURNED, preferred_element_type=F32)
    term = term + lax.dot_general(d_up, wu_ref[...], TURNED, preferred_element_type=F32)
    step = pl.program_id(0)

    @pl.when(step == 0)
    def _():
        total[...] = term

    @pl.when(step > 0)
    def _():
        total[...] += term

    @pl.when(step == pl.num_programs(0) - 1)
    def _():
        narrow = outs[0].shape[2]
        for z in range(plan.replicas):
            if plan.hops:
                index = jnp.bitwise_xor(where_ref[1], z)
                lanes = pl.ds(pl.multiple_of(index * narrow, 128), narrow)
            else:
                lanes = pl.ds(z * narrow, narrow)
            for x in range(plan.owners):
                at = z // 2 * plan.owners + x if plan.hops else z * plan.owners + x
                outs[z % len(outs)][at] = total[x * CAP : (x + 1) * CAP, lanes].astype(BF16)


def row_grads(plan, where, parts, wg, wu, wanted=1024):
    width, columns = wg.shape
    narrow = width // plan.replicas
    block = block_of(columns, wanted)
    strip = pl.BlockSpec((width, block), lambda i: (0, i))
    part_spec = pl.BlockSpec((plan.rows, block), lambda i: (0, i))
    sets = 2 if plan.hops else 1
    pieces = jax.ShapeDtypeStruct((plan.devices // sets, CAP, narrow), BF16)
    hidden = jax.ShapeDtypeStruct((plan.rows, columns), BF16)
    outs = pl.pallas_call(
        functools.partial(rows_kernel, plan),
        grid=(columns // block,),
        out_shape=[hidden] * 3 + [pieces] * sets,
        in_specs=[SMEM] + [part_spec] * 6 + [strip] * 2,
        out_specs=[part_spec] * 3 + [pl.BlockSpec(pieces.shape, lambda i: (0, 0, 0))] * sets,
        scratch_shapes=[pltpu.VMEM((plan.rows, width), F32)],
        compiler_params=params(48),
        cost_estimate=cost(4 * plan.rows * width * columns, 4 * width * columns),
        name="row_grads",
    )(where, *parts, wg, wu)
    return outs[:3], outs[3:]


def weights_kernel(factor, block, many, *refs):
    pairs = [(refs[2 * k], refs[2 * k + 1]) for k in range(many)]
    outs, done_ref, held, sems = refs[2 * many + 1 : 3 * many + 1], refs[-3], refs[-2], refs[-1]
    copies = []
    for i in range(held.shape[1]):
        cols = pl.ds(i * block, block)
        for k, (rows_ref, d_ref) in enumerate(pairs):
            grad = lax.dot_general(rows_ref[...], d_ref[:, cols], BOTH_FIRST, preferred_element_type=F32)
            held[k, i] = (grad * factor).astype(BF16)
            copy = pltpu.make_async_copy(held.at[k, i], outs[k].at[:, cols], sems.at[k, i])
            copy.start()
            copies.append(copy)
    done_ref[...] = jnp.zeros(done_ref.shape, F32)
    for copy in copies:
        copy.wait()


def weight_grads(factor, pairs, after, name, wanted=512):
    (rows, width), columns = pairs[0][0].shape, pairs[0][1].shape[1]
    block = block_of(columns, wanted)
    count, many = columns // block, len(pairs)
    return pl.pallas_call(
        functools.partial(weights_kernel, factor, block, many),
        out_shape=[jax.ShapeDtypeStruct((width, columns), BF16)] * many + [jax.ShapeDtypeStruct((8, 128), F32)],
        in_specs=[VMEM] * (2 * many) + [ANY],
        out_specs=[ANY] * many + [VMEM],
        scratch_shapes=[pltpu.VMEM((many, count, width, block), BF16), pltpu.SemaphoreType.DMA((many, count))],
        compiler_params=params(16 + 14 * many),
        cost_estimate=cost(2 * many * rows * width * columns, 2 * many * width * columns),
        name=name,
    )(*[array for pair in pairs for array in pair], after)


def pair_kernel(kept_ref, got_ref, after_ref, *outs):
    for at, out_ref in enumerate(outs):
        out_ref[0] = (kept_ref[at].astype(F32) + got_ref[at].astype(F32)).astype(BF16)


def pair_sum(kept, got, after):
    pieces, cap, narrow = kept.shape
    return pl.pallas_call(
        pair_kernel,
        out_shape=[jax.ShapeDtypeStruct((1, cap, narrow), BF16)] * pieces,
        in_specs=[VMEM, VMEM, ANY],
        out_specs=[VMEM] * pieces,
        compiler_params=params(8),
        name="pair_sum",
    )(kept, got, after)


def combine_kernel(plan, sel_ref, *refs):
    backs, out_ref = refs[:-1], refs[-1]
    total = jnp.zeros(out_ref.shape, F32)
    if plan.hops:
        for at in range(len(PARTNERS)):
            total = total + lax.dot_general(sel_ref[at], backs[at][0], BOTH_FIRST, preferred_element_type=F32)
    else:
        for z in range(plan.replicas):
            for x in range(plan.owners):
                chosen, piece = sel_ref[plan.expert_of(x, z)], backs[0][z * plan.owners + x]
                total = total + lax.dot_general(chosen, piece, BOTH_FIRST, preferred_element_type=F32)
    out_ref[...] = total.astype(BF16)


def combine(plan, sel, backs):
    count, narrow = sel.shape[2], backs[0].shape[2]
    return pl.pallas_call(
        functools.partial(combine_kernel, plan),
        out_shape=jax.ShapeDtypeStruct((count, narrow), BF16),
        in_specs=[VMEM] * (1 + len(backs)),
        out_specs=VMEM,
        compiler_params=params(8),
        name="combine",
    )(sel, *backs)


def body(mesh, tokens, cotangent, expert_ids, gate_values, gate_weight, up_weight, down_weight):
    plan = Plan(mesh, gate_weight.shape[1])
    where = jnp.stack((lax.axis_index("expert"), lax.axis_index("dp"))).astype(jnp.int32)
    wg, wu, wd = gate_weight, up_weight, down_weight

    def swap(part):
        size = mesh.shape["tensor"]
        return lax.ppermute(part, "tensor", [(i, i ^ 1) for i in range(size)])

    sel, sends = dispatch(plan, where, expert_ids, gate_values, tokens, cotangent, 6 * wg.size)
    if plan.hops:
        own, to_x, to_z, to_xz = sends
        far_x = plan.send(to_xz, 1, 0)
        far_own, near_own = plan.send(to_z, 0, 2), plan.send(own, 0, 1)
        from_x = plan.send(to_x, 1, 0)
        far_x, last_own = plan.send(far_x, 0, 2), plan.send(far_own, 0, 1)
        near_x = plan.send(from_x, 0, 1)
        last_x = plan.send(far_x, 0, 1)
        got = [own, from_x, near_own, near_x, far_own, far_x, last_own, last_x]
    else:
        got = [plan.scatter(sends[0])]
    q_full, part_h = forward(plan, where, got, 1, wd, "forward_h")
    other_h = swap(part_h)
    x_full, part_g = forward(plan, where, got, 0, wg, "forward_g")
    other_g = swap(part_g)
    (part_u,) = forward(plan, where, [x_full], None, wu, "forward_u")
    other_u = swap(part_u)
    parts = (part_g, other_g, part_u, other_u, part_h, other_h)
    factor = 1.0 / math.sqrt(tokens.shape[0] * plan.owners)
    (h, d_gate, d_up), pieces = row_grads(plan, where, parts, wg, wu)
    arrived = plan.send(pieces[1], 0, 1) if plan.hops else plan.scatter(pieces[0])
    grad_gate, grad_up, done = weight_grads(factor, ((x_full, d_gate), (x_full, d_up)), pieces[0], "grads_gu")
    if plan.hops:
        backs = pair_sum(pieces[0], arrived, done)
        backs = [plan.send(piece, *hop) if at else piece for at, (piece, hop) in enumerate(zip(backs, PARTNERS))]
        done = backs[0]
    else:
        backs = [arrived]
    grad_down, _ = weight_grads(factor, ((q_full, h),), done, "grad_down")
    token_grad = combine(plan, sel, backs)
    return (token_grad, grad_gate, grad_up, grad_down)


def solution(mesh):
    in_specs = (
        P(("groups", "expert"), ("tensor", "dp")),
        P(("groups", "expert"), ("tensor", "dp")),
        P(("groups", "expert"), None),
        P(("groups", "expert"), None),
        P("tensor", ("expert", "dp")),
        P("tensor", ("expert", "dp")),
        P("tensor", ("expert", "dp")),
    )
    out_specs = (
        P(("groups", "expert"), ("tensor", "dp")),
        P(("groups", "tensor"), ("expert", "dp")),
        P(("groups", "tensor"), ("expert", "dp")),
        P(("groups", "tensor"), ("expert", "dp")),
    )
    return jax.shard_map(
        functools.partial(body, mesh), mesh=mesh, in_specs=in_specs, out_specs=out_specs, check_vma=False
    )
```

```python
import functools
import math

import jax
import jax.numpy as jnp
from jax import lax
from jax.experimental import pallas as pl
from jax.experimental.pallas import tpu as pltpu
from jax.sharding import PartitionSpec as P

FF = 8192
EXPERTS = 4
CAP = 80
F32 = jnp.float32
BF16 = jnp.bfloat16
PARTNERS = ((0, 0), (1, 0), (0, 2), (1, 2))
TURNED = (((1,), (1,)), ((), ()))
BOTH_FIRST = (((0,), (0,)), ((), ()))
VMEM = pl.BlockSpec(memory_space=pltpu.VMEM)
ANY = pl.BlockSpec(memory_space=pl.ANY)


def params(mebibytes):
    return pltpu.CompilerParams(vmem_limit_bytes=mebibytes * 1024 * 1024)


def cost(flops, moved):
    return pl.CostEstimate(flops=flops, bytes_accessed=moved, transcendentals=0)


def block_of(size, wanted):
    while size % wanted:
        wanted //= 2
    return wanted


class Plan:
    def __init__(self, mesh, columns):
        self.owners = mesh.shape["expert"]
        self.replicas = mesh.shape["dp"]
        self.devices = self.owners * self.replicas
        self.rows = self.owners * CAP
        self.columns = columns
        self.hops = self.owners == 2 and self.replicas == 4 and 2 * columns == FF

    def expert_of(self, x, z):
        return (x * self.replicas + z) * self.columns // FF

    def send(self, array, dx, dz):
        pairs = []
        for x in range(self.owners):
            for z in range(self.replicas):
                pairs.append((z * self.owners + x, (z ^ dz) * self.owners + (x ^ dx)))
        return lax.ppermute(array, ("dp", "expert"), pairs)

    def scatter(self, array):
        return lax.all_to_all(array, ("dp", "expert"), 0, 0, tiled=True)


def dispatch_kernel(plan, *refs):
    sources, sel_ref, send_refs, held, sems = refs[:4], refs[4], refs[5:-5], refs[-5:-1], refs[-1]
    copies = [pltpu.make_async_copy(source, here, sems.at[k]) for k, (source, here) in enumerate(zip(sources, held))]
    for copy in copies:
        copy.start()
    for copy in copies:
        copy.wait()
    ids_ref, gates_ref, tok_ref, cot_ref = held
    count = tok_ref.shape[0]
    first, second = ids_ref[0:1, :], ids_ref[1:2, :]
    gate_first, gate_second = gates_ref[0:1, :].astype(F32), gates_ref[1:2, :].astype(F32)
    row = lax.broadcasted_iota(jnp.int32, (16, count), 0)
    named = ((row == first) | (row == second)).astype(F32)
    earlier = lax.broadcasted_iota(jnp.int32, (count, count), 0) < lax.broadcasted_iota(jnp.int32, (count, count), 1)
    before = jnp.dot(named.astype(BF16), earlier.astype(F32).astype(BF16), preferred_element_type=F32)
    slot = lax.broadcasted_iota(jnp.int32, (CAP, count), 0).astype(F32)

    def rows_for(expert):
        mine = row == expert
        position = jnp.sum(jnp.where(mine, before, 0.0), axis=0, keepdims=True)
        here = jnp.sum(jnp.where(mine, named, 0.0), axis=0, keepdims=True)
        chosen = jnp.where((position == slot) & (here > 0.5), 1.0, 0.0)
        gate = jnp.sum(chosen * jnp.where(first == expert, gate_first, gate_second), axis=1, keepdims=True)
        chosen = chosen.astype(BF16)
        x_rows = jnp.dot(chosen, tok_ref[...], preferred_element_type=F32).astype(BF16)
        q_rows = (gate * jnp.dot(chosen, cot_ref[...], preferred_element_type=F32)).astype(BF16)
        return chosen, x_rows, q_rows

    if plan.hops:
        for at, (dx, dz) in enumerate(PARTNERS):
            expert = plan.expert_of(jnp.bitwise_xor(lax.axis_index("expert"), dx), jnp.bitwise_xor(lax.axis_index("dp"), dz))
            sel_ref[at], send_refs[at][0, 0:CAP, :], send_refs[at][0, CAP : 2 * CAP, :] = rows_for(expert)
        return
    for expert in range(EXPERTS):
        chosen, x_rows, q_rows = rows_for(expert)
        sel_ref[expert] = chosen
        for z in range(plan.replicas):
            for x in range(plan.owners):
                if plan.expert_of(x, z) == expert:
                    send_refs[0][z * plan.owners + x, 0:CAP, :] = x_rows
                    send_refs[0][z * plan.owners + x, CAP : 2 * CAP, :] = q_rows


def dispatch(plan, ids, gates, tokens, cotangent):
    count, narrow = tokens.shape
    sends = [jax.ShapeDtypeStruct((1, 2 * CAP, narrow), BF16)] * len(PARTNERS)
    if not plan.hops:
        sends = [jax.ShapeDtypeStruct((plan.devices, 2 * CAP, narrow), BF16)]
    arrays = (ids.T, gates.T, tokens, cotangent)
    got = pl.pallas_call(
        functools.partial(dispatch_kernel, plan),
        out_shape=[jax.ShapeDtypeStruct((EXPERTS, CAP, count), BF16)] + sends,
        in_specs=[ANY] * 4,
        scratch_shapes=[pltpu.VMEM(array.shape, array.dtype) for array in arrays] + [pltpu.SemaphoreType.DMA((4,))],
        out_specs=[VMEM] * (1 + len(sends)),
        compiler_params=params(58),
        name="dispatch",
    )(*arrays)
    return got[0], got[1:]


def window_kernel(array_ref, *refs):
    refs[-1][...] = array_ref[...]


def window(array, after, fetched, name):
    return pl.pallas_call(
        window_kernel,
        out_shape=jax.ShapeDtypeStruct(array.shape, array.dtype),
        in_specs=[VMEM] + [ANY] * len(after),
        out_specs=VMEM,
        compiler_params=params(2),
        cost_estimate=cost(400 * fetched, fetched),
        name=name,
    )(array, *after)


def forward_kernel(plan, half, block, *refs):
    part_ref = refs[-1]
    if half is None:
        rows_ref, w_ref = refs[:2]
    else:
        pieces, w_ref, rows_ref = refs[:-3], refs[-3], refs[-2]
        narrow = pieces[0].shape[2]
        for z in range(plan.replicas):
            if plan.hops:
                index = jnp.bitwise_xor(lax.axis_index("dp"), z)
                lanes = pl.ds(pl.multiple_of(index * narrow, 128), narrow)
            else:
                lanes = pl.ds(z * narrow, narrow)
            for x in range(plan.owners):
                at = z * plan.owners + x
                piece = pieces[at] if plan.hops else pieces[0].at[pl.ds(at, 1)]
                rows_ref[x * CAP : (x + 1) * CAP, lanes] = piece[0, half * CAP : (half + 1) * CAP, :]
    for start in range(0, w_ref.shape[1], block):
        cols = pl.ds(start, block)
        part_ref[:, cols] = jnp.dot(rows_ref[...], w_ref[:, cols], preferred_element_type=F32).astype(BF16)


def forward(plan, rows_in, half, w, name, wanted=512):
    width, columns = w.shape
    block = block_of(columns, wanted)
    fresh = half is not None
    outs = [jax.ShapeDtypeStruct((plan.rows, width), BF16)] * fresh
    outs.append(jax.ShapeDtypeStruct((plan.rows, columns), BF16))
    return pl.pallas_call(
        functools.partial(forward_kernel, plan, half, block),
        out_shape=outs,
        in_specs=[VMEM] * (1 + len(rows_in)),
        out_specs=[VMEM] * len(outs),
        compiler_params=params(4),
        cost_estimate=cost(2 * plan.rows * width * columns, 8 * 1024 * 1024),
        name=name,
    )(*rows_in, w)


def rows_kernel(plan, g0, g1, u0, u1, d0, d1, wg_ref, wu_ref, h_ref, dg_ref, du_ref, *rest):
    outs, total = rest[:-1], rest[-1]
    gate = g0[...].astype(F32) + g1[...].astype(F32)
    up = u0[...].astype(F32) + u1[...].astype(F32)
    hidden = d0[...].astype(F32) + d1[...].astype(F32)
    sigma = jax.nn.sigmoid(gate)
    act = sigma * gate
    h_ref[...] = (act * up).astype(BF16)
    d_gate = (hidden * up * sigma * (1.0 + gate * (1.0 - sigma))).astype(BF16)
    d_up = (hidden * act).astype(BF16)
    dg_ref[...] = d_gate
    du_ref[...] = d_up
    term = lax.dot_general(wg_ref[...], d_gate, TURNED, preferred_element_type=F32)
    term = term + lax.dot_general(wu_ref[...], d_up, TURNED, preferred_element_type=F32)
    step = pl.program_id(0)

    @pl.when(step == 0)
    def _():
        total[...] = term

    @pl.when(step > 0)
    def _():
        total[...] += term

    @pl.when(step == pl.num_programs(0) - 1)
    def _():
        narrow = outs[0].shape[2]
        for z in range(plan.replicas):
            index = jnp.bitwise_xor(lax.axis_index("dp"), z) if plan.hops else z
            turned = total[pl.ds(pl.multiple_of(index * narrow, 32), narrow), :].T.astype(BF16)
            for x in range(plan.owners):
                at = z // 2 * plan.owners + x if plan.hops else z * plan.owners + x
                outs[z % len(outs)][at] = turned[x * CAP : (x + 1) * CAP, :]


def row_grads(plan, parts, wg, wu, wanted=1024):
    width, columns = wg.shape
    narrow = width // plan.replicas
    block = block_of(columns, wanted)
    strip = pl.BlockSpec((width, block), lambda i: (0, i))
    part_spec = pl.BlockSpec((plan.rows, block), lambda i: (0, i))
    sets = 2 if plan.hops else 1
    pieces = jax.ShapeDtypeStruct((plan.devices // sets, CAP, narrow), BF16)
    hidden = jax.ShapeDtypeStruct((plan.rows, columns), BF16)
    outs = pl.pallas_call(
        functools.partial(rows_kernel, plan),
        grid=(columns // block,),
        out_shape=[hidden] * 3 + [pieces] * sets,
        in_specs=[part_spec] * 6 + [strip] * 2,
        out_specs=[part_spec] * 3 + [pl.BlockSpec(pieces.shape, lambda i: (0, 0, 0))] * sets,
        scratch_shapes=[pltpu.VMEM((width, plan.rows), F32)],
        compiler_params=params(32),
        cost_estimate=cost(4 * plan.rows * width * columns, 4 * width * columns),
        name="row_grads",
    )(*parts, wg, wu)
    return outs[:3], outs[3:]


def weights_kernel(factor, block, many, *refs):
    pairs = [(refs[2 * k], refs[2 * k + 1]) for k in range(many)]
    outs, done_ref, held, sems = refs[2 * many + 1 : 3 * many + 1], refs[-3], refs[-2], refs[-1]
    copies = []
    for i in range(held.shape[1]):
        cols = pl.ds(i * block, block)
        for k, (rows_ref, d_ref) in enumerate(pairs):
            grad = lax.dot_general(rows_ref[...], d_ref[:, cols], BOTH_FIRST, preferred_element_type=F32)
            held[k, i] = (grad * factor).astype(BF16)
            copy = pltpu.make_async_copy(held.at[k, i], outs[k].at[:, cols], sems.at[k, i])
            copy.start()
            copies.append(copy)
    done_ref[...] = jnp.zeros(done_ref.shape, F32)
    for copy in copies:
        copy.wait()


def weight_grads(factor, pairs, after, name, wanted=512):
    (rows, width), columns = pairs[0][0].shape, pairs[0][1].shape[1]
    block = block_of(columns, wanted)
    count, many = columns // block, len(pairs)
    return pl.pallas_call(
        functools.partial(weights_kernel, factor, block, many),
        out_shape=[jax.ShapeDtypeStruct((width, columns), BF16)] * many + [jax.ShapeDtypeStruct((8, 128), F32)],
        in_specs=[VMEM] * (2 * many) + [ANY],
        out_specs=[ANY] * many + [VMEM],
        scratch_shapes=[pltpu.VMEM((many, count, width, block), BF16), pltpu.SemaphoreType.DMA((many, count))],
        compiler_params=params(16 + 14 * many),
        cost_estimate=cost(2 * many * rows * width * columns, 2 * many * width * columns),
        name=name,
    )(*[array for pair in pairs for array in pair], after)


def pair_kernel(kept_ref, got_ref, after_ref, *outs):
    for at, out_ref in enumerate(outs):
        out_ref[0] = (kept_ref[at].astype(F32) + got_ref[at].astype(F32)).astype(BF16)


def pair_sum(kept, got, after):
    pieces, cap, narrow = kept.shape
    return pl.pallas_call(
        pair_kernel,
        out_shape=[jax.ShapeDtypeStruct((1, cap, narrow), BF16)] * pieces,
        in_specs=[VMEM, VMEM, ANY],
        out_specs=[VMEM] * pieces,
        compiler_params=params(8),
        name="pair_sum",
    )(kept, got, after)


def combine_kernel(plan, sel_ref, *refs):
    backs, out_ref = refs[:-1], refs[-1]
    total = jnp.zeros(out_ref.shape, F32)
    if plan.hops:
        for at in range(len(PARTNERS)):
            total = total + lax.dot_general(sel_ref[at], backs[at][0], BOTH_FIRST, preferred_element_type=F32)
    else:
        for z in range(plan.replicas):
            for x in range(plan.owners):
                chosen, piece = sel_ref[plan.expert_of(x, z)], backs[0][z * plan.owners + x]
                total = total + lax.dot_general(chosen, piece, BOTH_FIRST, preferred_element_type=F32)
    out_ref[...] = total.astype(BF16)


def combine(plan, sel, backs):
    count, narrow = sel.shape[2], backs[0].shape[2]
    return pl.pallas_call(
        functools.partial(combine_kernel, plan),
        out_shape=jax.ShapeDtypeStruct((count, narrow), BF16),
        in_specs=[VMEM] * (1 + len(backs)),
        out_specs=VMEM,
        compiler_params=params(8),
        name="combine",
    )(sel, *backs)


def body(mesh, tokens, cotangent, expert_ids, gate_values, gate_weight, up_weight, down_weight):
    plan = Plan(mesh, gate_weight.shape[1])
    wg, wu, wd = gate_weight, up_weight, down_weight

    def swap(part):
        size = mesh.shape["tensor"]
        return lax.ppermute(part, "tensor", [(i, i ^ 1) for i in range(size)])

    sel, sends = dispatch(plan, expert_ids, gate_values, tokens, cotangent)
    if plan.hops:
        own, to_x, to_z, to_xz = sends
        own = window(own, (), 4 * wg.size, "window_own")
        to_x = window(to_x, (own,), 8 * wg.size, "window_side")
        far_own, far_x = plan.send(to_z, 0, 2), plan.send(to_xz, 1, 2)
        near_own, near_x = plan.send(own, 0, 1), plan.send(to_x, 1, 1)
        from_x = plan.send(to_x, 1, 0)
        last_own, last_x = plan.send(far_own, 0, 1), plan.send(far_x, 0, 1)
        got = [own, from_x, near_own, near_x, far_own, far_x, last_own, last_x]
    else:
        got = [plan.scatter(sends[0])]
    q_full, part_h = forward(plan, got, 1, wd, "forward_h")
    other_h = swap(part_h)
    x_full, part_g = forward(plan, got, 0, wg, "forward_g")
    other_g = swap(part_g)
    (part_u,) = forward(plan, [x_full], None, wu, "forward_u")
    other_u = swap(part_u)
    parts = (part_g, other_g, part_u, other_u, part_h, other_h)
    factor = 1.0 / math.sqrt(tokens.shape[0] * plan.owners)
    (h, d_gate, d_up), pieces = row_grads(plan, parts, wg, wu)
    arrived = plan.send(pieces[1], 0, 1) if plan.hops else plan.scatter(pieces[0])
    grad_gate, grad_up, done = weight_grads(factor, ((x_full, d_gate), (x_full, d_up)), pieces[0], "grads_gu")
    if plan.hops:
        backs = pair_sum(pieces[0], arrived, done)
        backs = [plan.send(piece, *hop) if at else piece for at, (piece, hop) in enumerate(zip(backs, PARTNERS))]
        done = backs[0]
    else:
        backs = [arrived]
    grad_down, _ = weight_grads(factor, ((q_full, h),), done, "grad_down")
    token_grad = combine(plan, sel, backs)
    return (token_grad, grad_gate, grad_up, grad_down)


def solution(mesh):
    in_specs = (
        P(("groups", "expert"), ("tensor", "dp")),
        P(("groups", "expert"), ("tensor", "dp")),
        P(("groups", "expert"), None),
        P(("groups", "expert"), None),
        P("tensor", ("expert", "dp")),
        P("tensor", ("expert", "dp")),
        P("tensor", ("expert", "dp")),
    )
    out_specs = (
        P(("groups", "expert"), ("tensor", "dp")),
        P(("groups", "tensor"), ("expert", "dp")),
        P(("groups", "tensor"), ("expert", "dp")),
        P(("groups", "tensor"), ("expert", "dp")),
    )
    return jax.shard_map(
        functools.partial(body, mesh), mesh=mesh, in_specs=in_specs, out_specs=out_specs, check_vma=False
    )
```

```python
import functools
import math

import jax
import jax.numpy as jnp
from jax import lax
from jax.experimental import pallas as pl
from jax.experimental.pallas import tpu as pltpu
from jax.sharding import PartitionSpec as P

FF = 8192
EXPERTS = 4
CAP = 80
F32 = jnp.float32
BF16 = jnp.bfloat16
PARTNERS = ((0, 0), (1, 0), (0, 2), (1, 2))
TURNED = (((1,), (1,)), ((), ()))
BOTH_FIRST = (((0,), (0,)), ((), ()))
VMEM = pl.BlockSpec(memory_space=pltpu.VMEM)
ANY = pl.BlockSpec(memory_space=pl.ANY)


def params(mebibytes):
    return pltpu.CompilerParams(vmem_limit_bytes=mebibytes * 1024 * 1024)


def cost(flops, moved):
    return pl.CostEstimate(flops=flops, bytes_accessed=moved, transcendentals=0)


def block_of(size, wanted):
    while size % wanted:
        wanted //= 2
    return wanted


class Plan:
    def __init__(self, mesh, columns):
        self.owners = mesh.shape["expert"]
        self.replicas = mesh.shape["dp"]
        self.devices = self.owners * self.replicas
        self.rows = self.owners * CAP
        self.columns = columns
        self.hops = self.owners == 2 and self.replicas == 4 and 2 * columns == FF

    def expert_of(self, x, z):
        return (x * self.replicas + z) * self.columns // FF

    def send(self, array, dx, dz):
        pairs = []
        for x in range(self.owners):
            for z in range(self.replicas):
                pairs.append((z * self.owners + x, (z ^ dz) * self.owners + (x ^ dx)))
        return lax.ppermute(array, ("dp", "expert"), pairs)

    def scatter(self, array):
        return lax.all_to_all(array, ("dp", "expert"), 0, 0, tiled=True)


def dispatch_kernel(plan, *refs):
    sources, sel_ref, send_refs, held, sems = refs[:4], refs[4], refs[5:-5], refs[-5:-1], refs[-1]
    copies = [pltpu.make_async_copy(source, here, sems.at[k]) for k, (source, here) in enumerate(zip(sources, held))]
    for copy in copies:
        copy.start()
    for copy in copies:
        copy.wait()
    ids_ref, gates_ref, tok_ref, cot_ref = held
    count = tok_ref.shape[0]
    first, second = ids_ref[0:1, :], ids_ref[1:2, :]
    gate_first, gate_second = gates_ref[0:1, :].astype(F32), gates_ref[1:2, :].astype(F32)
    row = lax.broadcasted_iota(jnp.int32, (16, count), 0)
    named = ((row == first) | (row == second)).astype(F32)
    earlier = lax.broadcasted_iota(jnp.int32, (count, count), 0) < lax.broadcasted_iota(jnp.int32, (count, count), 1)
    before = jnp.dot(named.astype(BF16), earlier.astype(F32).astype(BF16), preferred_element_type=F32)
    slot = lax.broadcasted_iota(jnp.int32, (CAP, count), 0).astype(F32)

    def rows_for(expert):
        mine = row == expert
        position = jnp.sum(jnp.where(mine, before, 0.0), axis=0, keepdims=True)
        here = jnp.sum(jnp.where(mine, named, 0.0), axis=0, keepdims=True)
        chosen = jnp.where((position == slot) & (here > 0.5), 1.0, 0.0)
        gate = jnp.sum(chosen * jnp.where(first == expert, gate_first, gate_second), axis=1, keepdims=True)
        chosen = chosen.astype(BF16)
        x_rows = jnp.dot(chosen, tok_ref[...], preferred_element_type=F32).astype(BF16)
        q_rows = (gate * jnp.dot(chosen, cot_ref[...], preferred_element_type=F32)).astype(BF16)
        return chosen, x_rows, q_rows

    if plan.hops:
        for at, (dx, dz) in enumerate(PARTNERS):
            expert = plan.expert_of(jnp.bitwise_xor(lax.axis_index("expert"), dx), jnp.bitwise_xor(lax.axis_index("dp"), dz))
            sel_ref[at], send_refs[at][0, 0:CAP, :], send_refs[at][0, CAP : 2 * CAP, :] = rows_for(expert)
        return
    for expert in range(EXPERTS):
        chosen, x_rows, q_rows = rows_for(expert)
        sel_ref[expert] = chosen
        for z in range(plan.replicas):
            for x in range(plan.owners):
                if plan.expert_of(x, z) == expert:
                    send_refs[0][z * plan.owners + x, 0:CAP, :] = x_rows
                    send_refs[0][z * plan.owners + x, CAP : 2 * CAP, :] = q_rows


def dispatch(plan, ids, gates, tokens, cotangent):
    count, narrow = tokens.shape
    sends = [jax.ShapeDtypeStruct((1, 2 * CAP, narrow), BF16)] * len(PARTNERS)
    if not plan.hops:
        sends = [jax.ShapeDtypeStruct((plan.devices, 2 * CAP, narrow), BF16)]
    arrays = (ids.T, gates.T, tokens, cotangent)
    got = pl.pallas_call(
        functools.partial(dispatch_kernel, plan),
        out_shape=[jax.ShapeDtypeStruct((EXPERTS, CAP, count), BF16)] + sends,
        in_specs=[ANY] * 4,
        scratch_shapes=[pltpu.VMEM(array.shape, array.dtype) for array in arrays] + [pltpu.SemaphoreType.DMA((4,))],
        out_specs=[VMEM] * (1 + len(sends)),
        compiler_params=params(58),
        name="dispatch",
    )(*arrays)
    return got[0], got[1:]


def window_kernel(array_ref, *refs):
    refs[-1][...] = array_ref[...]


def window(array, after, fetched, name):
    return pl.pallas_call(
        window_kernel,
        out_shape=jax.ShapeDtypeStruct(array.shape, array.dtype),
        in_specs=[VMEM] + [ANY] * len(after),
        out_specs=VMEM,
        compiler_params=params(2),
        cost_estimate=cost(400 * fetched, fetched),
        name=name,
    )(array, *after)


def forward_kernel(plan, half, after, block, *refs):
    refs = refs[after:]
    part_ref = refs[-1]
    if half is None:
        rows_ref, w_ref = refs[:2]
    else:
        pieces, w_ref, rows_ref = refs[:-3], refs[-3], refs[-2]
        narrow = pieces[0].shape[2]
        for z in range(plan.replicas):
            if plan.hops:
                index = jnp.bitwise_xor(lax.axis_index("dp"), z)
                lanes = pl.ds(pl.multiple_of(index * narrow, 128), narrow)
            else:
                lanes = pl.ds(z * narrow, narrow)
            for x in range(plan.owners):
                at = z * plan.owners + x
                piece = pieces[at] if plan.hops else pieces[0].at[pl.ds(at, 1)]
                rows_ref[x * CAP : (x + 1) * CAP, lanes] = piece[0, half * CAP : (half + 1) * CAP, :]
    for start in range(0, w_ref.shape[1], block):
        cols = pl.ds(start, block)
        part_ref[:, cols] = jnp.dot(rows_ref[...], w_ref[:, cols], preferred_element_type=F32).astype(BF16)


def forward(plan, rows_in, half, w, after, name, wanted=512):
    width, columns = w.shape
    block = block_of(columns, wanted)
    fresh = half is not None
    outs = [jax.ShapeDtypeStruct((plan.rows, width), BF16)] * fresh
    outs.append(jax.ShapeDtypeStruct((plan.rows, columns), BF16))
    return pl.pallas_call(
        functools.partial(forward_kernel, plan, half, len(after), block),
        out_shape=outs,
        in_specs=[ANY] * len(after) + [VMEM] * (1 + len(rows_in)),
        out_specs=[VMEM] * len(outs),
        compiler_params=params(4),
        cost_estimate=cost(2 * plan.rows * width * columns // 1, 8 * 1024 * 1024 // 1),
        name=name,
    )(*after, *rows_in, w)


def act_kernel(block, g0, g1, u0, u1, h_ref, by_gate_ref, by_up_ref):
    for start in range(0, g0.shape[1], block):
        cols = pl.ds(start, block)
        gate = g0[:, cols].astype(F32) + g1[:, cols].astype(F32)
        up = u0[:, cols].astype(F32) + u1[:, cols].astype(F32)
        sigma = jax.nn.sigmoid(gate)
        act = sigma * gate
        h_ref[:, cols] = (act * up).astype(BF16)
        by_gate_ref[:, cols] = (up * sigma * (1.0 + gate * (1.0 - sigma))).astype(BF16)
        by_up_ref[:, cols] = act.astype(BF16)


def activations(parts, wanted=256):
    rows, columns = parts[0].shape
    return pl.pallas_call(
        functools.partial(act_kernel, block_of(columns, wanted)),
        out_shape=[jax.ShapeDtypeStruct((rows, columns), BF16)] * 3,
        in_specs=[VMEM] * 4,
        out_specs=[VMEM] * 3,
        compiler_params=params(4),
        cost_estimate=cost(9000 * rows * columns, 14 * rows * columns),
        name="activations",
    )(*parts)


def rows_kernel(plan, by_gate_ref, by_up_ref, d0, d1, wg_ref, wu_ref, dg_ref, du_ref, *rest):
    outs, total = rest[:-1], rest[-1]
    hidden = d0[...].astype(F32) + d1[...].astype(F32)
    d_gate = (hidden * by_gate_ref[...].astype(F32)).astype(BF16)
    d_up = (hidden * by_up_ref[...].astype(F32)).astype(BF16)
    dg_ref[...] = d_gate
    du_ref[...] = d_up
    step, block = pl.program_id(0), d_gate.shape[1]
    cols = pl.ds(pl.multiple_of(step * block, block), block)
    term = lax.dot_general(wg_ref[:, cols], d_gate, TURNED, preferred_element_type=F32)
    term = term + lax.dot_general(wu_ref[:, cols], d_up, TURNED, preferred_element_type=F32)
    step = pl.program_id(0)

    @pl.when(step == 0)
    def _():
        total[...] = term

    @pl.when(step > 0)
    def _():
        total[...] += term

    @pl.when(step == pl.num_programs(0) - 1)
    def _():
        narrow = outs[0].shape[2]
        for z in range(plan.replicas):
            index = jnp.bitwise_xor(lax.axis_index("dp"), z) if plan.hops else z
            turned = total[pl.ds(pl.multiple_of(index * narrow, 32), narrow), :].T.astype(BF16)
            for x in range(plan.owners):
                at = z // 2 * plan.owners + x if plan.hops else z * plan.owners + x
                outs[z % len(outs)][at] = turned[x * CAP : (x + 1) * CAP, :]


def row_grads(plan, parts, wg, wu, wanted=1024):
    width, columns = wg.shape
    narrow = width // plan.replicas
    block = block_of(columns, wanted)
    strip = VMEM
    part_spec = pl.BlockSpec((plan.rows, block), lambda i: (0, i))
    sets = 2 if plan.hops else 1
    pieces = jax.ShapeDtypeStruct((plan.devices // sets, CAP, narrow), BF16)
    hidden = jax.ShapeDtypeStruct((plan.rows, columns), BF16)
    outs = pl.pallas_call(
        functools.partial(rows_kernel, plan),
        grid=(columns // block,),
        out_shape=[hidden] * 2 + [pieces] * sets,
        in_specs=[part_spec] * 4 + [strip] * 2,
        out_specs=[part_spec] * 2 + [pl.BlockSpec(pieces.shape, lambda i: (0, 0, 0))] * sets,
        scratch_shapes=[pltpu.VMEM((width, plan.rows), F32)],
        compiler_params=params(14),
        cost_estimate=cost(4 * plan.rows * width * columns, 4 * width * columns),
        name="row_grads",
    )(*parts, wg, wu)
    return outs[:2], outs[2:]


def weights_kernel(factor, block, many, *refs):
    pairs = [(refs[2 * k], refs[2 * k + 1]) for k in range(many)]
    outs, done_ref, held, sems = refs[2 * many + 1 : 3 * many + 1], refs[-3], refs[-2], refs[-1]
    copies = []
    for i in range(held.shape[1]):
        cols = pl.ds(i * block, block)
        for k, (rows_ref, d_ref) in enumerate(pairs):
            grad = lax.dot_general(rows_ref[...], d_ref[:, cols], BOTH_FIRST, preferred_element_type=F32)
            held[k, i] = (grad * factor).astype(BF16)
            copy = pltpu.make_async_copy(held.at[k, i], outs[k].at[:, cols], sems.at[k, i])
            copy.start()
            copies.append(copy)
    done_ref[...] = jnp.zeros(done_ref.shape, F32)
    for copy in copies:
        copy.wait()


def weight_grads(factor, pairs, after, name, wanted=512):
    (rows, width), columns = pairs[0][0].shape, pairs[0][1].shape[1]
    block = block_of(columns, wanted)
    count, many = columns // block, len(pairs)
    return pl.pallas_call(
        functools.partial(weights_kernel, factor, block, many),
        out_shape=[jax.ShapeDtypeStruct((width, columns), BF16)] * many + [jax.ShapeDtypeStruct((8, 128), F32)],
        in_specs=[VMEM] * (2 * many) + [ANY],
        out_specs=[ANY] * many + [VMEM],
        scratch_shapes=[pltpu.VMEM((many, count, width, block), BF16), pltpu.SemaphoreType.DMA((many, count))],
        compiler_params=params(16 + 14 * many),
        cost_estimate=cost(2 * many * rows * width * columns, 2 * many * width * columns),
        name=name,
    )(*[array for pair in pairs for array in pair], after)


def pair_kernel(kept_ref, got_ref, after_ref, *outs):
    for at, out_ref in enumerate(outs):
        out_ref[0] = (kept_ref[at].astype(F32) + got_ref[at].astype(F32)).astype(BF16)


def pair_sum(kept, got, after):
    pieces, cap, narrow = kept.shape
    return pl.pallas_call(
        pair_kernel,
        out_shape=[jax.ShapeDtypeStruct((1, cap, narrow), BF16)] * pieces,
        in_specs=[VMEM, VMEM, ANY],
        out_specs=[VMEM] * pieces,
        compiler_params=params(8),
        name="pair_sum",
    )(kept, got, after)


def combine_kernel(plan, sel_ref, *refs):
    backs, out_ref = refs[:-1], refs[-1]
    total = jnp.zeros(out_ref.shape, F32)
    if plan.hops:
        for at in range(len(PARTNERS)):
            total = total + lax.dot_general(sel_ref[at], backs[at][0], BOTH_FIRST, preferred_element_type=F32)
    else:
        for z in range(plan.replicas):
            for x in range(plan.owners):
                chosen, piece = sel_ref[plan.expert_of(x, z)], backs[0][z * plan.owners + x]
                total = total + lax.dot_general(chosen, piece, BOTH_FIRST, preferred_element_type=F32)
    out_ref[...] = total.astype(BF16)


def combine(plan, sel, backs):
    count, narrow = sel.shape[2], backs[0].shape[2]
    return pl.pallas_call(
        functools.partial(combine_kernel, plan),
        out_shape=jax.ShapeDtypeStruct((count, narrow), BF16),
        in_specs=[VMEM] * (1 + len(backs)),
        out_specs=VMEM,
        compiler_params=params(8),
        name="combine",
    )(sel, *backs)


def body(mesh, tokens, cotangent, expert_ids, gate_values, gate_weight, up_weight, down_weight):
    plan = Plan(mesh, gate_weight.shape[1])
    wg, wu, wd = gate_weight, up_weight, down_weight

    def swap(part):
        size = mesh.shape["tensor"]
        return lax.ppermute(part, "tensor", [(i, i ^ 1) for i in range(size)])

    sel, sends = dispatch(plan, expert_ids, gate_values, tokens, cotangent)
    if plan.hops:
        own, to_x, to_z, to_xz = sends
        to_x = window(to_x, (), 4 * wg.size, "window_first")
        to_x = window(to_x, (), 8 * wg.size, "window_second")
        far_own, far_x = plan.send(to_z, 0, 2), plan.send(to_xz, 1, 2)
        near_own, near_x = plan.send(own, 0, 1), plan.send(to_x, 1, 1)
        from_x = plan.send(to_x, 1, 0)
        last_own, last_x = plan.send(far_own, 0, 1), plan.send(far_x, 0, 1)
        got = [own, from_x, near_own, near_x, far_own, far_x, last_own, last_x]
    else:
        got = [plan.scatter(sends[0])]
    x_full, part_g = forward(plan, got, 0, wg, (), "forward_g")
    other_g = swap(part_g)
    (part_u,) = forward(plan, [x_full], None, wu, (), "forward_u")
    other_u = swap(part_u)
    q_full, part_h = forward(plan, got, 1, wd, (other_g,), "forward_h")
    other_h = swap(part_h)
    h, by_gate, by_up = activations((part_g, other_g, part_u, other_u))
    parts = (by_gate, by_up, part_h, other_h)
    factor = 1.0 / math.sqrt(tokens.shape[0] * plan.owners)
    (d_gate, d_up), pieces = row_grads(plan, parts, wg, wu)
    arrived = plan.send(pieces[1], 0, 1) if plan.hops else plan.scatter(pieces[0])
    grad_gate, grad_up, done = weight_grads(factor, ((x_full, d_gate), (x_full, d_up)), pieces[0], "grads_gu")
    if plan.hops:
        backs = pair_sum(pieces[0], arrived, done)
        backs = [plan.send(piece, *hop) if at else piece for at, (piece, hop) in enumerate(zip(backs, PARTNERS))]
        done = backs[0]
    else:
        backs = [arrived]
    grad_down, _ = weight_grads(factor, ((q_full, h),), done, "grad_down")
    token_grad = combine(plan, sel, backs)
    return (token_grad, grad_gate, grad_up, grad_down)


def solution(mesh):
    in_specs = (
        P(("groups", "expert"), ("tensor", "dp")),
        P(("groups", "expert"), ("tensor", "dp")),
        P(("groups", "expert"), None),
        P(("groups", "expert"), None),
        P("tensor", ("expert", "dp")),
        P("tensor", ("expert", "dp")),
        P("tensor", ("expert", "dp")),
    )
    out_specs = (
        P(("groups", "expert"), ("tensor", "dp")),
        P(("groups", "tensor"), ("expert", "dp")),
        P(("groups", "tensor"), ("expert", "dp")),
        P(("groups", "tensor"), ("expert", "dp")),
    )
    return jax.shard_map(
        functools.partial(body, mesh), mesh=mesh, in_specs=in_specs, out_specs=out_specs, check_vma=False
    )
```

```python
import functools
import math

import jax
import jax.numpy as jnp
from jax import lax
from jax.experimental import pallas as pl
from jax.experimental.pallas import tpu as pltpu
from jax.sharding import PartitionSpec as P

FF = 8192
EXPERTS = 4
CAP = 80
F32 = jnp.float32
BF16 = jnp.bfloat16
PARTNERS = ((0, 0), (1, 0), (0, 2), (1, 2))
TURNED = (((1,), (1,)), ((), ()))
BOTH_FIRST = (((0,), (0,)), ((), ()))
VMEM = pl.BlockSpec(memory_space=pltpu.VMEM)
ANY = pl.BlockSpec(memory_space=pl.ANY)


def params(mebibytes):
    return pltpu.CompilerParams(vmem_limit_bytes=mebibytes * 1024 * 1024)


def cost(flops, moved):
    return pl.CostEstimate(flops=flops, bytes_accessed=moved, transcendentals=0)


def block_of(size, wanted):
    while size % wanted:
        wanted //= 2
    return wanted


class Plan:
    def __init__(self, mesh, columns):
        self.owners = mesh.shape["expert"]
        self.replicas = mesh.shape["dp"]
        self.devices = self.owners * self.replicas
        self.rows = self.owners * CAP
        self.columns = columns
        self.hops = self.owners == 2 and self.replicas == 4 and 2 * columns == FF

    def expert_of(self, x, z):
        return (x * self.replicas + z) * self.columns // FF

    def send(self, array, dx, dz):
        pairs = []
        for x in range(self.owners):
            for z in range(self.replicas):
                pairs.append((z * self.owners + x, (z ^ dz) * self.owners + (x ^ dx)))
        return lax.ppermute(array, ("dp", "expert"), pairs)

    def scatter(self, array):
        return lax.all_to_all(array, ("dp", "expert"), 0, 0, tiled=True)


def dispatch_kernel(plan, *refs):
    sources, sel_ref, send_refs, held, sems = refs[:4], refs[4], refs[5:-5], refs[-5:-1], refs[-1]
    copies = [pltpu.make_async_copy(source, here, sems.at[k]) for k, (source, here) in enumerate(zip(sources, held))]
    for copy in copies:
        copy.start()
    for copy in copies:
        copy.wait()
    ids_ref, gates_ref, tok_ref, cot_ref = held
    count = tok_ref.shape[0]
    first, second = ids_ref[0:1, :], ids_ref[1:2, :]
    gate_first, gate_second = gates_ref[0:1, :].astype(F32), gates_ref[1:2, :].astype(F32)
    row = lax.broadcasted_iota(jnp.int32, (16, count), 0)
    named = ((row == first) | (row == second)).astype(F32)
    earlier = lax.broadcasted_iota(jnp.int32, (count, count), 0) < lax.broadcasted_iota(jnp.int32, (count, count), 1)
    before = jnp.dot(named.astype(BF16), earlier.astype(F32).astype(BF16), preferred_element_type=F32)
    slot = lax.broadcasted_iota(jnp.int32, (CAP, count), 0).astype(F32)

    def rows_for(expert):
        mine = row == expert
        position = jnp.sum(jnp.where(mine, before, 0.0), axis=0, keepdims=True)
        here = jnp.sum(jnp.where(mine, named, 0.0), axis=0, keepdims=True)
        chosen = jnp.where((position == slot) & (here > 0.5), 1.0, 0.0)
        gate = jnp.sum(chosen * jnp.where(first == expert, gate_first, gate_second), axis=1, keepdims=True)
        chosen = chosen.astype(BF16)
        x_rows = jnp.dot(chosen, tok_ref[...], preferred_element_type=F32).astype(BF16)
        q_rows = (gate * jnp.dot(chosen, cot_ref[...], preferred_element_type=F32)).astype(BF16)
        return chosen, x_rows, q_rows

    if plan.hops:
        for at, (dx, dz) in enumerate(PARTNERS):
            expert = plan.expert_of(jnp.bitwise_xor(lax.axis_index("expert"), dx), jnp.bitwise_xor(lax.axis_index("dp"), dz))
            sel_ref[at], send_refs[at][0, 0:CAP, :], send_refs[at][0, CAP : 2 * CAP, :] = rows_for(expert)
        return
    for expert in range(EXPERTS):
        chosen, x_rows, q_rows = rows_for(expert)
        sel_ref[expert] = chosen
        for z in range(plan.replicas):
            for x in range(plan.owners):
                if plan.expert_of(x, z) == expert:
                    send_refs[0][z * plan.owners + x, 0:CAP, :] = x_rows
                    send_refs[0][z * plan.owners + x, CAP : 2 * CAP, :] = q_rows


def dispatch(plan, ids, gates, tokens, cotangent):
    count, narrow = tokens.shape
    sends = [jax.ShapeDtypeStruct((1, 2 * CAP, narrow), BF16)] * len(PARTNERS)
    if not plan.hops:
        sends = [jax.ShapeDtypeStruct((plan.devices, 2 * CAP, narrow), BF16)]
    arrays = (ids.T, gates.T, tokens, cotangent)
    got = pl.pallas_call(
        functools.partial(dispatch_kernel, plan),
        out_shape=[jax.ShapeDtypeStruct((EXPERTS, CAP, count), BF16)] + sends,
        in_specs=[ANY] * 4,
        scratch_shapes=[pltpu.VMEM(array.shape, array.dtype) for array in arrays] + [pltpu.SemaphoreType.DMA((4,))],
        out_specs=[VMEM] * (1 + len(sends)),
        compiler_params=params(58),
        name="dispatch",
    )(*arrays)
    return got[0], got[1:]


def window_kernel(array_ref, *refs):
    refs[-1][...] = array_ref[...]


def window(array, after, fetched, name):
    return pl.pallas_call(
        window_kernel,
        out_shape=jax.ShapeDtypeStruct(array.shape, array.dtype),
        in_specs=[VMEM] + [ANY] * len(after),
        out_specs=VMEM,
        compiler_params=params(2),
        cost_estimate=cost(400 * fetched, fetched),
        name=name,
    )(array, *after)


def forward_kernel(plan, half, after, block, *refs):
    refs = refs[after:]
    part_ref = refs[-1]
    if half is None:
        rows_ref, w_ref = refs[:2]
    else:
        pieces, w_ref, rows_ref = refs[:-3], refs[-3], refs[-2]
        narrow = pieces[0].shape[2]
        for z in range(plan.replicas):
            if plan.hops:
                index = jnp.bitwise_xor(lax.axis_index("dp"), z)
                lanes = pl.ds(pl.multiple_of(index * narrow, 128), narrow)
            else:
                lanes = pl.ds(z * narrow, narrow)
            for x in range(plan.owners):
                at = z * plan.owners + x
                piece = pieces[at] if plan.hops else pieces[0].at[pl.ds(at, 1)]
                rows_ref[x * CAP : (x + 1) * CAP, lanes] = piece[0, half * CAP : (half + 1) * CAP, :]
    for start in range(0, w_ref.shape[1], block):
        cols = pl.ds(start, block)
        part_ref[:, cols] = jnp.dot(rows_ref[...], w_ref[:, cols], preferred_element_type=F32).astype(BF16)


def forward(plan, rows_in, half, w, after, name, wanted=512):
    width, columns = w.shape
    block = block_of(columns, wanted)
    fresh = half is not None
    outs = [jax.ShapeDtypeStruct((plan.rows, width), BF16)] * fresh
    outs.append(jax.ShapeDtypeStruct((plan.rows, columns), BF16))
    return pl.pallas_call(
        functools.partial(forward_kernel, plan, half, len(after), block),
        out_shape=outs,
        in_specs=[ANY] * len(after) + [VMEM] * (1 + len(rows_in)),
        out_specs=[VMEM] * len(outs),
        compiler_params=params(4),
        cost_estimate=cost(2 * plan.rows * width * columns // 1, 8 * 1024 * 1024 // 1),
        name=name,
    )(*after, *rows_in, w)


def act_kernel(block, g0, g1, u0, u1, h_ref, by_gate_ref, by_up_ref):
    for start in range(0, g0.shape[1], block):
        cols = pl.ds(start, block)
        gate = g0[:, cols].astype(F32) + g1[:, cols].astype(F32)
        up = u0[:, cols].astype(F32) + u1[:, cols].astype(F32)
        sigma = jax.nn.sigmoid(gate)
        act = sigma * gate
        h_ref[:, cols] = (act * up).astype(BF16)
        by_gate_ref[:, cols] = (up * sigma * (1.0 + gate * (1.0 - sigma))).astype(BF16)
        by_up_ref[:, cols] = act.astype(BF16)


def activations(parts, wanted=256):
    rows, columns = parts[0].shape
    return pl.pallas_call(
        functools.partial(act_kernel, block_of(columns, wanted)),
        out_shape=[jax.ShapeDtypeStruct((rows, columns), BF16)] * 3,
        in_specs=[VMEM] * 4,
        out_specs=[VMEM] * 3,
        compiler_params=params(4),
        cost_estimate=cost(9000 * rows * columns, 14 * rows * columns),
        name="activations",
    )(*parts)


def rows_kernel(plan, block, by_gate_ref, by_up_ref, d0, d1, wg_ref, wu_ref, dg_ref, du_ref, *rest):
    outs, total = rest[:-1], rest[-1]
    for start in range(0, wg_ref.shape[1], block):
        cols = pl.ds(start, block)
        hidden = d0[:, cols].astype(F32) + d1[:, cols].astype(F32)
        d_gate = (hidden * by_gate_ref[:, cols].astype(F32)).astype(BF16)
        d_up = (hidden * by_up_ref[:, cols].astype(F32)).astype(BF16)
        dg_ref[:, cols] = d_gate
        du_ref[:, cols] = d_up
        term = lax.dot_general(wg_ref[:, cols], d_gate, TURNED, preferred_element_type=F32)
        term = term + lax.dot_general(wu_ref[:, cols], d_up, TURNED, preferred_element_type=F32)
        total[...] = term if start == 0 else total[...] + term
    narrow = outs[0].shape[2]
    for z in range(plan.replicas):
        index = jnp.bitwise_xor(lax.axis_index("dp"), z) if plan.hops else z
        turned = total[pl.ds(pl.multiple_of(index * narrow, 32), narrow), :].T.astype(BF16)
        for x in range(plan.owners):
            at = z // 2 * plan.owners + x if plan.hops else z * plan.owners + x
            outs[z % len(outs)][at] = turned[x * CAP : (x + 1) * CAP, :]


def row_grads(plan, parts, wg, wu, wanted=2048):
    width, columns = wg.shape
    narrow = width // plan.replicas
    sets = 2 if plan.hops else 1
    pieces = jax.ShapeDtypeStruct((plan.devices // sets, CAP, narrow), BF16)
    hidden = jax.ShapeDtypeStruct((plan.rows, columns), BF16)
    outs = pl.pallas_call(
        functools.partial(rows_kernel, plan, block_of(columns, wanted)),
        out_shape=[hidden] * 2 + [pieces] * sets,
        in_specs=[VMEM] * 6,
        out_specs=[VMEM] * (2 + sets),
        scratch_shapes=[pltpu.VMEM((width, plan.rows), F32)],
        compiler_params=params(12),
        cost_estimate=cost(4 * plan.rows * width * columns, 4 * width * columns),
        name="row_grads",
    )(*parts, wg, wu)
    return outs[:2], outs[2:]


def weights_kernel(factor, block, many, *refs):
    pairs = [(refs[2 * k], refs[2 * k + 1]) for k in range(many)]
    outs, done_ref, held, sems = refs[2 * many + 1 : 3 * many + 1], refs[-3], refs[-2], refs[-1]
    copies = []
    for i in range(held.shape[1]):
        cols = pl.ds(i * block, block)
        for k, (rows_ref, d_ref) in enumerate(pairs):
            grad = lax.dot_general(rows_ref[...], d_ref[:, cols], BOTH_FIRST, preferred_element_type=F32)
            held[k, i] = (grad * factor).astype(BF16)
            copy = pltpu.make_async_copy(held.at[k, i], outs[k].at[:, cols], sems.at[k, i])
            copy.start()
            copies.append(copy)
    done_ref[...] = jnp.zeros(done_ref.shape, F32)
    for copy in copies:
        copy.wait()


def weight_grads(factor, pairs, after, name, wanted=512):
    (rows, width), columns = pairs[0][0].shape, pairs[0][1].shape[1]
    block = block_of(columns, wanted)
    count, many = columns // block, len(pairs)
    return pl.pallas_call(
        functools.partial(weights_kernel, factor, block, many),
        out_shape=[jax.ShapeDtypeStruct((width, columns), BF16)] * many + [jax.ShapeDtypeStruct((8, 128), F32)],
        in_specs=[VMEM] * (2 * many) + [ANY],
        out_specs=[ANY] * many + [VMEM],
        scratch_shapes=[pltpu.VMEM((many, count, width, block), BF16), pltpu.SemaphoreType.DMA((many, count))],
        compiler_params=params(16 + 14 * many),
        cost_estimate=cost(2 * many * rows * width * columns, 2 * many * width * columns),
        name=name,
    )(*[array for pair in pairs for array in pair], after)


def pair_kernel(kept_ref, got_ref, after_ref, *outs):
    for at, out_ref in enumerate(outs):
        out_ref[0] = (kept_ref[at].astype(F32) + got_ref[at].astype(F32)).astype(BF16)


def pair_sum(kept, got, after):
    pieces, cap, narrow = kept.shape
    return pl.pallas_call(
        pair_kernel,
        out_shape=[jax.ShapeDtypeStruct((1, cap, narrow), BF16)] * pieces,
        in_specs=[VMEM, VMEM, ANY],
        out_specs=[VMEM] * pieces,
        compiler_params=params(8),
        name="pair_sum",
    )(kept, got, after)


def combine_kernel(plan, sel_ref, *refs):
    backs, out_ref = refs[:-1], refs[-1]
    total = jnp.zeros(out_ref.shape, F32)
    if plan.hops:
        for at in range(len(PARTNERS)):
            total = total + lax.dot_general(sel_ref[at], backs[at][0], BOTH_FIRST, preferred_element_type=F32)
    else:
        for z in range(plan.replicas):
            for x in range(plan.owners):
                chosen, piece = sel_ref[plan.expert_of(x, z)], backs[0][z * plan.owners + x]
                total = total + lax.dot_general(chosen, piece, BOTH_FIRST, preferred_element_type=F32)
    out_ref[...] = total.astype(BF16)


def combine(plan, sel, backs):
    count, narrow = sel.shape[2], backs[0].shape[2]
    return pl.pallas_call(
        functools.partial(combine_kernel, plan),
        out_shape=jax.ShapeDtypeStruct((count, narrow), BF16),
        in_specs=[VMEM] * (1 + len(backs)),
        out_specs=VMEM,
        compiler_params=params(8),
        name="combine",
    )(sel, *backs)


def body(mesh, tokens, cotangent, expert_ids, gate_values, gate_weight, up_weight, down_weight):
    plan = Plan(mesh, gate_weight.shape[1])
    wg, wu, wd = gate_weight, up_weight, down_weight

    def swap(part):
        size = mesh.shape["tensor"]
        return lax.ppermute(part, "tensor", [(i, i ^ 1) for i in range(size)])

    sel, sends = dispatch(plan, expert_ids, gate_values, tokens, cotangent)
    if plan.hops:
        own, to_x, to_z, to_xz = sends
        to_x = window(to_x, (), 4 * wg.size, "window_first")
        to_x = window(to_x, (), 8 * wg.size, "window_second")
        far_own, far_x = plan.send(to_z, 0, 2), plan.send(to_xz, 1, 2)
        near_own, near_x = plan.send(own, 0, 1), plan.send(to_x, 1, 1)
        from_x = plan.send(to_x, 1, 0)
        last_own, last_x = plan.send(far_own, 0, 1), plan.send(far_x, 0, 1)
        got = [own, from_x, near_own, near_x, far_own, far_x, last_own, last_x]
    else:
        got = [plan.scatter(sends[0])]
    x_full, part_g = forward(plan, got, 0, wg, (), "forward_g")
    other_g = swap(part_g)
    (part_u,) = forward(plan, [x_full], None, wu, (), "forward_u")
    other_u = swap(part_u)
    q_full, part_h = forward(plan, got, 1, wd, (other_g,), "forward_h")
    other_h = swap(part_h)
    h, by_gate, by_up = activations((part_g, other_g, part_u, other_u))
    parts = (by_gate, by_up, part_h, other_h)
    factor = 1.0 / math.sqrt(tokens.shape[0] * plan.owners)
    (d_gate, d_up), pieces = row_grads(plan, parts, wg, wu)
    arrived = plan.send(pieces[1], 0, 1) if plan.hops else plan.scatter(pieces[0])
    grad_gate, grad_up, done = weight_grads(factor, ((x_full, d_gate), (x_full, d_up)), pieces[0], "grads_gu")
    if plan.hops:
        backs = pair_sum(pieces[0], arrived, done)
        backs = [plan.send(piece, *hop) if at else piece for at, (piece, hop) in enumerate(zip(backs, PARTNERS))]
        done = backs[0]
    else:
        backs = [arrived]
    grad_down, _ = weight_grads(factor, ((q_full, h),), done, "grad_down")
    token_grad = combine(plan, sel, backs)
    return (token_grad, grad_gate, grad_up, grad_down)


def solution(mesh):
    in_specs = (
        P(("groups", "expert"), ("tensor", "dp")),
        P(("groups", "expert"), ("tensor", "dp")),
        P(("groups", "expert"), None),
        P(("groups", "expert"), None),
        P("tensor", ("expert", "dp")),
        P("tensor", ("expert", "dp")),
        P("tensor", ("expert", "dp")),
    )
    out_specs = (
        P(("groups", "expert"), ("tensor", "dp")),
        P(("groups", "tensor"), ("expert", "dp")),
        P(("groups", "tensor"), ("expert", "dp")),
        P(("groups", "tensor"), ("expert", "dp")),
    )
    return jax.shard_map(
        functools.partial(body, mesh), mesh=mesh, in_specs=in_specs, out_specs=out_specs, check_vma=False
    )
```

```python
import functools
import math

import jax
import jax.numpy as jnp
from jax import lax
from jax.experimental import pallas as pl
from jax.experimental.pallas import tpu as pltpu
from jax.sharding import PartitionSpec as P

FF = 8192
EXPERTS = 4
CAP = 80
F32 = jnp.float32
BF16 = jnp.bfloat16
PARTNERS = ((0, 0), (1, 0), (0, 2), (1, 2))
TURNED = (((1,), (1,)), ((), ()))
BOTH_FIRST = (((0,), (0,)), ((), ()))
VMEM = pl.BlockSpec(memory_space=pltpu.VMEM)
ANY = pl.BlockSpec(memory_space=pl.ANY)


def params(mebibytes):
    return pltpu.CompilerParams(vmem_limit_bytes=mebibytes * 1024 * 1024)


def cost(flops, moved):
    return pl.CostEstimate(flops=flops, bytes_accessed=moved, transcendentals=0)


def block_of(size, wanted):
    while size % wanted:
        wanted //= 2
    return wanted


class Plan:
    def __init__(self, mesh, columns):
        self.owners = mesh.shape["expert"]
        self.replicas = mesh.shape["dp"]
        self.devices = self.owners * self.replicas
        self.rows = self.owners * CAP
        self.columns = columns
        self.hops = self.owners == 2 and self.replicas == 4 and 2 * columns == FF

    def expert_of(self, x, z):
        return (x * self.replicas + z) * self.columns // FF

    def send(self, array, dx, dz):
        pairs = []
        for x in range(self.owners):
            for z in range(self.replicas):
                pairs.append((z * self.owners + x, (z ^ dz) * self.owners + (x ^ dx)))
        return lax.ppermute(array, ("dp", "expert"), pairs)

    def scatter(self, array):
        return lax.all_to_all(array, ("dp", "expert"), 0, 0, tiled=True)


def dispatch_kernel(plan, *refs):
    sources, sel_ref, send_refs, held, sems = refs[:4], refs[4], refs[5:-5], refs[-5:-1], refs[-1]
    copies = [pltpu.make_async_copy(source, here, sems.at[k]) for k, (source, here) in enumerate(zip(sources, held))]
    for copy in copies:
        copy.start()
    for copy in copies:
        copy.wait()
    ids_ref, gates_ref, tok_ref, cot_ref = held
    count = tok_ref.shape[0]
    first, second = ids_ref[0:1, :], ids_ref[1:2, :]
    gate_first, gate_second = gates_ref[0:1, :].astype(F32), gates_ref[1:2, :].astype(F32)
    row = lax.broadcasted_iota(jnp.int32, (16, count), 0)
    named = ((row == first) | (row == second)).astype(F32)
    earlier = lax.broadcasted_iota(jnp.int32, (count, count), 0) < lax.broadcasted_iota(jnp.int32, (count, count), 1)
    before = jnp.dot(named.astype(BF16), earlier.astype(F32).astype(BF16), preferred_element_type=F32)
    slot = lax.broadcasted_iota(jnp.int32, (CAP, count), 0).astype(F32)

    def rows_for(expert):
        mine = row == expert
        position = jnp.sum(jnp.where(mine, before, 0.0), axis=0, keepdims=True)
        here = jnp.sum(jnp.where(mine, named, 0.0), axis=0, keepdims=True)
        chosen = jnp.where((position == slot) & (here > 0.5), 1.0, 0.0)
        gate = jnp.sum(chosen * jnp.where(first == expert, gate_first, gate_second), axis=1, keepdims=True)
        chosen = chosen.astype(BF16)
        x_rows = jnp.dot(chosen, tok_ref[...], preferred_element_type=F32).astype(BF16)
        q_rows = (gate * jnp.dot(chosen, cot_ref[...], preferred_element_type=F32)).astype(BF16)
        return chosen, x_rows, q_rows

    if plan.hops:
        for at, (dx, dz) in enumerate(PARTNERS):
            expert = plan.expert_of(jnp.bitwise_xor(lax.axis_index("expert"), dx), jnp.bitwise_xor(lax.axis_index("dp"), dz))
            sel_ref[at], send_refs[at][0, 0:CAP, :], send_refs[at][0, CAP : 2 * CAP, :] = rows_for(expert)
        return
    for expert in range(EXPERTS):
        chosen, x_rows, q_rows = rows_for(expert)
        sel_ref[expert] = chosen
        for z in range(plan.replicas):
            for x in range(plan.owners):
                if plan.expert_of(x, z) == expert:
                    send_refs[0][z * plan.owners + x, 0:CAP, :] = x_rows
                    send_refs[0][z * plan.owners + x, CAP : 2 * CAP, :] = q_rows


def dispatch(plan, ids, gates, tokens, cotangent):
    count, narrow = tokens.shape
    sends = [jax.ShapeDtypeStruct((1, 2 * CAP, narrow), BF16)] * len(PARTNERS)
    if not plan.hops:
        sends = [jax.ShapeDtypeStruct((plan.devices, 2 * CAP, narrow), BF16)]
    arrays = (ids.T, gates.T, tokens, cotangent)
    got = pl.pallas_call(
        functools.partial(dispatch_kernel, plan),
        out_shape=[jax.ShapeDtypeStruct((EXPERTS, CAP, count), BF16)] + sends,
        in_specs=[ANY] * 4,
        scratch_shapes=[pltpu.VMEM(array.shape, array.dtype) for array in arrays] + [pltpu.SemaphoreType.DMA((4,))],
        out_specs=[VMEM] * (1 + len(sends)),
        compiler_params=params(58),
        name="dispatch",
    )(*arrays)
    return got[0], got[1:]


def window_kernel(array_ref, *refs):
    refs[-1][...] = array_ref[...]


def window(array, after, fetched, name):
    return pl.pallas_call(
        window_kernel,
        out_shape=jax.ShapeDtypeStruct(array.shape, array.dtype),
        in_specs=[VMEM] + [ANY] * len(after),
        out_specs=VMEM,
        compiler_params=params(2),
        cost_estimate=cost(400 * fetched, fetched),
        name=name,
    )(array, *after)


def forward_kernel(plan, half, after, block, *refs):
    refs = refs[after:]
    part_ref = refs[-1]
    if half is None:
        rows_ref, w_ref = refs[:2]
    else:
        pieces, w_ref, rows_ref = refs[:-3], refs[-3], refs[-2]
        narrow = pieces[0].shape[2]
        for z in range(plan.replicas):
            if plan.hops:
                index = jnp.bitwise_xor(lax.axis_index("dp"), z)
                lanes = pl.ds(pl.multiple_of(index * narrow, 128), narrow)
            else:
                lanes = pl.ds(z * narrow, narrow)
            for x in range(plan.owners):
                at = z * plan.owners + x
                piece = pieces[at] if plan.hops else pieces[0].at[pl.ds(at, 1)]
                rows_ref[x * CAP : (x + 1) * CAP, lanes] = piece[0, half * CAP : (half + 1) * CAP, :]
    for start in range(0, w_ref.shape[1], block):
        cols = pl.ds(start, block)
        part_ref[:, cols] = jnp.dot(rows_ref[...], w_ref[:, cols], preferred_element_type=F32).astype(BF16)


def forward(plan, rows_in, half, w, after, name, wanted=512):
    width, columns = w.shape
    block = block_of(columns, wanted)
    fresh = half is not None
    outs = [jax.ShapeDtypeStruct((plan.rows, width), BF16)] * fresh
    outs.append(jax.ShapeDtypeStruct((plan.rows, columns), BF16))
    return pl.pallas_call(
        functools.partial(forward_kernel, plan, half, len(after), block),
        out_shape=outs,
        in_specs=[ANY] * len(after) + [VMEM] * (1 + len(rows_in)),
        out_specs=[VMEM] * len(outs),
        compiler_params=params(4),
        cost_estimate=cost(2 * plan.rows * width * columns // 1, 8 * 1024 * 1024 // 1),
        name=name,
    )(*after, *rows_in, w)


def act_kernel(block, g0, g1, u0, u1, h_ref, by_gate_ref, by_up_ref):
    for start in range(0, g0.shape[1], block):
        cols = pl.ds(start, block)
        gate = g0[:, cols].astype(F32) + g1[:, cols].astype(F32)
        up = u0[:, cols].astype(F32) + u1[:, cols].astype(F32)
        sigma = jax.nn.sigmoid(gate)
        act = sigma * gate
        h_ref[:, cols] = (act * up).astype(BF16)
        by_gate_ref[:, cols] = (up * sigma * (1.0 + gate * (1.0 - sigma))).astype(BF16)
        by_up_ref[:, cols] = act.astype(BF16)


def activations(parts, wanted=256):
    rows, columns = parts[0].shape
    return pl.pallas_call(
        functools.partial(act_kernel, block_of(columns, wanted)),
        out_shape=[jax.ShapeDtypeStruct((rows, columns), BF16)] * 3,
        in_specs=[VMEM] * 4,
        out_specs=[VMEM] * 3,
        compiler_params=params(4),
        cost_estimate=cost(9000 * rows * columns, 14 * rows * columns),
        name="activations",
    )(*parts)


def rows_kernel(plan, block, by_gate_ref, by_up_ref, d0, d1, wg_ref, wu_ref, dg_ref, du_ref, *rest):
    outs, total = rest[:-1], rest[-1]
    for start in range(0, wg_ref.shape[1], block):
        cols = pl.ds(start, block)
        hidden = d0[:, cols].astype(F32) + d1[:, cols].astype(F32)
        d_gate = (hidden * by_gate_ref[:, cols].astype(F32)).astype(BF16)
        d_up = (hidden * by_up_ref[:, cols].astype(F32)).astype(BF16)
        dg_ref[:, cols] = d_gate
        du_ref[:, cols] = d_up
        term = lax.dot_general(wg_ref[:, cols], d_gate, TURNED, preferred_element_type=F32)
        term = term + lax.dot_general(wu_ref[:, cols], d_up, TURNED, preferred_element_type=F32)
        total[...] = term if start == 0 else total[...] + term
    narrow = outs[0].shape[2]
    for z in range(plan.replicas):
        index = jnp.bitwise_xor(lax.axis_index("dp"), z) if plan.hops else z
        turned = total[pl.ds(pl.multiple_of(index * narrow, 32), narrow), :].T.astype(BF16)
        for x in range(plan.owners):
            at = z // 2 * plan.owners + x if plan.hops else z * plan.owners + x
            outs[z % len(outs)][at] = turned[x * CAP : (x + 1) * CAP, :]


def row_grads(plan, parts, wg, wu, wanted=2048):
    width, columns = wg.shape
    narrow = width // plan.replicas
    sets = 2 if plan.hops else 1
    pieces = jax.ShapeDtypeStruct((plan.devices // sets, CAP, narrow), BF16)
    hidden = jax.ShapeDtypeStruct((plan.rows, columns), BF16)
    outs = pl.pallas_call(
        functools.partial(rows_kernel, plan, block_of(columns, wanted)),
        out_shape=[hidden] * 2 + [pieces] * sets,
        in_specs=[VMEM] * 6,
        out_specs=[VMEM] * (2 + sets),
        scratch_shapes=[pltpu.VMEM((width, plan.rows), F32)],
        compiler_params=params(12),
        cost_estimate=cost(4 * plan.rows * width * columns, 4 * width * columns),
        name="row_grads",
    )(*parts, wg, wu)
    return outs[:2], outs[2:]


def weights_kernel(factor, block, many, *refs):
    pairs = [(refs[2 * k], refs[2 * k + 1]) for k in range(many)]
    outs, done_ref, held, sems = refs[2 * many + 1 : 3 * many + 1], refs[-3], refs[-2], refs[-1]
    copies = []
    for i in range(held.shape[1]):
        cols = pl.ds(i * block, block)
        for k, (rows_ref, d_ref) in enumerate(pairs):
            grad = lax.dot_general(rows_ref[...], d_ref[:, cols], BOTH_FIRST, preferred_element_type=F32)
            held[k, i] = (grad * factor).astype(BF16)
            copy = pltpu.make_async_copy(held.at[k, i], outs[k].at[:, cols], sems.at[k, i])
            copy.start()
            copies.append(copy)
    done_ref[...] = jnp.zeros(done_ref.shape, F32)
    for copy in copies:
        copy.wait()


def weight_grads(factor, pairs, after, name, wanted=512):
    (rows, width), columns = pairs[0][0].shape, pairs[0][1].shape[1]
    block = block_of(columns, wanted)
    count, many = columns // block, len(pairs)
    return pl.pallas_call(
        functools.partial(weights_kernel, factor, block, many),
        out_shape=[jax.ShapeDtypeStruct((width, columns), BF16)] * many + [jax.ShapeDtypeStruct((8, 128), F32)],
        in_specs=[VMEM] * (2 * many) + [ANY],
        out_specs=[ANY] * many + [VMEM],
        scratch_shapes=[pltpu.VMEM((many, count, width, block), BF16), pltpu.SemaphoreType.DMA((many, count))],
        compiler_params=params(16 + 14 * many),
        cost_estimate=cost(2 * many * rows * width * columns, 2 * many * width * columns),
        name=name,
    )(*[array for pair in pairs for array in pair], after)


def pair_kernel(kept_ref, got_ref, after_ref, *outs):
    for at, out_ref in enumerate(outs):
        out_ref[0] = (kept_ref[at].astype(F32) + got_ref[at].astype(F32)).astype(BF16)


def pair_sum(kept, got, after):
    pieces, cap, narrow = kept.shape
    return pl.pallas_call(
        pair_kernel,
        out_shape=[jax.ShapeDtypeStruct((1, cap, narrow), BF16)] * pieces,
        in_specs=[VMEM, VMEM, ANY],
        out_specs=[VMEM] * pieces,
        compiler_params=params(8),
        name="pair_sum",
    )(kept, got, after)


def combine_kernel(plan, sel_ref, *refs):
    backs, out_ref = refs[:-1], refs[-1]
    total = jnp.zeros(out_ref.shape, F32)
    if plan.hops:
        for at in range(len(PARTNERS)):
            total = total + lax.dot_general(sel_ref[at], backs[at][0], BOTH_FIRST, preferred_element_type=F32)
    else:
        for z in range(plan.replicas):
            for x in range(plan.owners):
                chosen, piece = sel_ref[plan.expert_of(x, z)], backs[0][z * plan.owners + x]
                total = total + lax.dot_general(chosen, piece, BOTH_FIRST, preferred_element_type=F32)
    out_ref[...] = total.astype(BF16)


def combine(plan, sel, backs):
    count, narrow = sel.shape[2], backs[0].shape[2]
    return pl.pallas_call(
        functools.partial(combine_kernel, plan),
        out_shape=jax.ShapeDtypeStruct((count, narrow), BF16),
        in_specs=[VMEM] * (1 + len(backs)),
        out_specs=VMEM,
        compiler_params=params(8),
        name="combine",
    )(sel, *backs)


def body(mesh, tokens, cotangent, expert_ids, gate_values, gate_weight, up_weight, down_weight):
    plan = Plan(mesh, gate_weight.shape[1])
    wg, wu, wd = gate_weight, up_weight, down_weight

    def swap(part):
        size = mesh.shape["tensor"]
        return lax.ppermute(part, "tensor", [(i, i ^ 1) for i in range(size)])

    sel, sends = dispatch(plan, expert_ids, gate_values, tokens, cotangent)
    if plan.hops:
        own, to_x, to_z, to_xz = sends
        to_x = window(to_x, (), 4 * wg.size, "window_first")
        to_x = window(to_x, (), 8 * wg.size, "window_second")
        far_own, far_x = plan.send(to_z, 0, 2), plan.send(to_xz, 1, 2)
        near_own, near_x = plan.send(own, 0, 1), plan.send(to_x, 1, 1)
        from_x = plan.send(to_x, 1, 0)
        last_own, last_x = plan.send(far_own, 0, 1), plan.send(far_x, 0, 1)
        got = [own, from_x, near_own, near_x, far_own, far_x, last_own, last_x]
    else:
        got = [plan.scatter(sends[0])]
    x_full, part_g = forward(plan, got, 0, wg, (), "forward_g")
    other_g = swap(part_g)
    (part_u,) = forward(plan, [x_full], None, wu, (), "forward_u")
    other_u = swap(part_u)
    q_full, part_h = forward(plan, got, 1, wd, (other_g,), "forward_h")
    other_h = swap(part_h)
    h, by_gate, by_up = activations((part_g, other_g, part_u, other_u))
    parts = (by_gate, by_up, part_h, other_h)
    factor = 1.0 / math.sqrt(tokens.shape[0] * plan.owners)
    (d_gate, d_up), pieces = row_grads(plan, parts, wg, wu)
    arrived = plan.send(pieces[1], 0, 1) if plan.hops else plan.scatter(pieces[0])
    grad_gate, grad_up, done = weight_grads(factor, ((x_full, d_gate), (x_full, d_up)), pieces[0], "grads_gu")
    if plan.hops:
        backs = pair_sum(pieces[0], arrived, done)
        backs = [plan.send(piece, *hop) if at else piece for at, (piece, hop) in enumerate(zip(backs, PARTNERS))]
        done = backs[0]
    else:
        backs = [arrived]
    grad_down, _ = weight_grads(factor, ((q_full, h),), done, "grad_down", 256)
    token_grad = combine(plan, sel, backs)
    return (token_grad, grad_gate, grad_up, grad_down)


def solution(mesh):
    in_specs = (
        P(("groups", "expert"), ("tensor", "dp")),
        P(("groups", "expert"), ("tensor", "dp")),
        P(("groups", "expert"), None),
        P(("groups", "expert"), None),
        P("tensor", ("expert", "dp")),
        P("tensor", ("expert", "dp")),
        P("tensor", ("expert", "dp")),
    )
    out_specs = (
        P(("groups", "expert"), ("tensor", "dp")),
        P(("groups", "tensor"), ("expert", "dp")),
        P(("groups", "tensor"), ("expert", "dp")),
        P(("groups", "tensor"), ("expert", "dp")),
    )
    return jax.shard_map(
        functools.partial(body, mesh), mesh=mesh, in_specs=in_specs, out_specs=out_specs, check_vma=False
    )
```
